128 devices in a mesh: tile: 16 (over x, z), inf: 8 (over y, core).
Axes of the slice: x: 4, y: 4, z: 4, core: 2. Of those that a mesh axis runs over, the one named last changes fastest.
Arguments:
- u_field: float32 [64, 1024, 1024], P(None, 'tile', 'inf'), may hold values from -6 to 6
- v_field: float32 [64, 1024, 1024], P(None, 'tile', 'inf'), may hold values from -6 to 6
- diffusivity: float32 [1024, 1024], P('tile', 'inf'), may hold values from 0.03 to 0.24
- active_columns: int32 [262144], P(('tile', 'inf')), may hold values from 0 to 8191, as said below
- regimes: int32 [262144, 1], P(('tile', 'inf')), may hold values from 0 to 127; in each aligned block of 2048 rows (0 to 2047, 2048 to 4095, ...) at most 32 rows name the same one
- first_layer: float32 [128, 128, 256], P(('tile', 'inf')), may hold values from -0.5 to 0.5
- second_layer: float32 [128, 256, 256], P(('tile', 'inf')), may hold values from -0.375 to 0.375
- third_layer: float32 [128, 256, 256], P(('tile', 'inf')), may hold values from -0.375 to 0.375
- last_layer: float32 [128, 256, 128], P(('tile', 'inf')), may hold values from -0.375 to 0.375
Outputs:
- u_next: float32 [64, 1024, 1024], P(None, 'tile', 'inf')
- v_next: float32 [64, 1024, 1024], P(None, 'tile', 'inf')
The draws below stay inside these ranges and needn't reach their ends.
Inputs may be any that keep to these rules, and one draw needn't show every extreme that they name: `active_columns`: the 2048 entries of one device are distinct flat indices x * 128 + y of columns of its own tile. `regimes`: among the rows of one device no network is named more than 32 times.
All inputs are finite; a program needn't handle non-finite values.
Results may differ from the reference program's by a relative error of at most 0.0003.
Values sent between devices are 32-bit elements; how exact they have to be, the bound alone decides.
A program may use at most 128 MiB of HBM per device.

```python
import math
import jax
import jax.numpy as jnp
import numpy as np
from jax import lax

LEV = 64
HID = 256
PASSES = 4
CY = 128
CX = 64
A_DEV = 2048
CAP = 32
EXPERTS = 128
ACT = 262144
NX = 1024
NY = 1024
N_INF = 8


def draw_active_columns(key, part):
    blocks = ACT // A_DEV
    keys = jax.random.split(jax.random.fold_in(key, 7), blocks)

    def one_block(block_key):
        return jax.random.permutation(block_key, CX * CY)[:A_DEV]
    return jax.vmap(one_block)(keys).reshape(-1).astype(jnp.int32)


def shard_levels(stream_key, dims, pieces, least, high):
    level, own = 1.0, jax.random.fold_in(stream_key, 6)
    for position, parts in pieces:
        draws = jnp.exp(jax.random.uniform(jax.random.fold_in(own, position), (parts,), jnp.float32, least / len(pieces), high / len(pieces)))
        level = level * jnp.repeat(draws, dims[position] // parts).reshape([-1 if axis == position else 1 for axis in range(len(dims))])
    return level


def routed_block(key, own, number, rows, amount, top, bound, skew):
    order = jax.random.permutation(key, amount)
    heavy_load, usual = portions_of(amount, rows * top, bound, skew, True), portions_of(amount, rows * top, bound, skew, False)
    places = jnp.arange(amount)

    def named(tallies, rotation):
        used = int((tallies > 0).sum())
        fixed = max(1, used // 4)
        passed = fixed + (places - fixed + rotation * (used - fixed)) % max(1, amount - fixed)
        return jnp.zeros((amount,), jnp.int32).at[order[jnp.where(places < fixed, places, passed)]].set(jnp.asarray(tallies, jnp.int32))

    tallies = jnp.where(number % 4 == 0, named(heavy_load, number // 4), named(usual, number - number // 4 - 1))
    mixed = jax.random.permutation(jax.random.fold_in(own, 3), amount)
    giver, sink = mixed[0:amount // 2 * 2:2], mixed[1:amount // 2 * 2:2]
    slack = jnp.minimum(tallies[giver] - 1, bound - tallies[sink]) // 2
    slack = jnp.where((giver == order[0]) | (sink == order[0]) | (tallies[sink] == 0), 0, jnp.maximum(slack, 0))
    passed = jax.random.randint(jax.random.fold_in(own, 4), (amount // 2,), 0, 1 << 20) % (slack + 1)
    tallies = tallies.at[giver].add(-passed).at[sink].add(passed)
    items = jnp.searchsorted(jnp.cumsum(tallies), jnp.arange(rows * top), side="right").astype(jnp.int32)
    grid = items.reshape(top, rows).T
    grid = grid[jax.random.permutation(jax.random.fold_in(own, 1), rows)]
    rotation = jax.random.randint(jax.random.fold_in(own, 2), (rows, 1), 0, top)
    return jnp.take_along_axis(grid, (jnp.arange(top)[None, :] + rotation) % top, axis=1)


def portions_of(amount, total, limit, lean, full):
    portions = [(1 << 20) // math.isqrt(standing ** lean) + 1 for standing in range(1, amount + 1)]
    largest = limit if full else min(limit, max(-(-total // amount), total * portions[0] // sum(portions)))
    least = 1 if total - largest >= amount - 1 else 0
    holding, surplus = [largest] + [least] * (amount - 1), total - largest - least * (amount - 1)
    while surplus > 0:
        free = [i for i in range(1, amount) if holding[i] < largest] or [i for i in range(1, amount) if holding[i] < limit]
        mass, budget = sum([portions[i] for i in free]), surplus
        for i in free:
            more = min(limit - holding[i], max(1, budget * portions[i] // mass), surplus)
            holding[i] = holding[i] + more
            surplus = surplus - more
    return np.array(holding)


def centred(own_key, shape, deviation, limit, shards=(), held_as=jnp.bfloat16):
    drawn = jax.random.normal(own_key, shape, jnp.float32) * deviation
    if len(shards) > 0:
        drawn = shard_levels(own_key, shape, shards, -0.22, 0.18) * drawn
    return jnp.clip(drawn, min=-limit, max=limit).astype(held_as)


def setup_inputs(seed: int = 0) -> dict:
    key_of = jax.random.split(jax.random.key(seed), 10)
    u_field = centred(key_of[0], (LEV, NX, NY), 1.0, 6.0, ((1, 16), (2, 8)), jnp.float32)
    v_field = centred(key_of[1], (LEV, NX, NY), 1.0, 6.0, ((1, 16), (2, 8)), jnp.float32)
    diffusivity = jnp.clip(jnp.exp(math.log(0.24) - 2.0794415 * jax.random.uniform(key_of[2], (NX, NY), jnp.float32) ** shard_levels(key_of[2], (NX, NY), ((0, 16), (1, 8)), -0.2, 0.2)), 0.03, 0.24)
    active_columns = draw_active_columns(jax.random.fold_in(key_of[9], 71), 0)
    regimes_keys = jax.random.split(jax.random.fold_in(key_of[4], 1), ACT // A_DEV)
    regimes_turns = jax.random.permutation(jax.random.fold_in(key_of[4], 3), ACT // A_DEV)
    regimes = jax.vmap(lambda own, number: routed_block(jax.random.fold_in(key_of[4], 2), own, number, A_DEV, EXPERTS, 1, CAP, 2))(regimes_keys, regimes_turns).reshape((ACT, 1))
    first_layer = centred(key_of[5], (EXPERTS, 2 * LEV, HID), (2 * LEV) ** -0.5, 0.5, ((0, 128),), jnp.float32)
    second_layer = centred(key_of[6], (EXPERTS, HID, HID), HID ** -0.5, 0.375, ((0, 128),), jnp.float32)
    third_layer = centred(key_of[7], (EXPERTS, HID, HID), HID ** -0.5, 0.375, ((0, 128),), jnp.float32)
    last_layer = centred(key_of[8], (EXPERTS, HID, 2 * LEV), HID ** -0.5, 0.375, ((0, 128),), jnp.float32)
    return {"u_field": u_field, "v_field": v_field, "diffusivity": diffusivity, "active_columns": active_columns, "regimes": regimes, "first_layer": first_layer, "second_layer": second_layer, "third_layer": third_layer, "last_layer": last_layer}


def standardize(rows):
    center = lax.optimization_barrier(jnp.mean(rows, axis=-1, keepdims=True))
    spread = lax.optimization_barrier(jnp.mean(jnp.square(rows - center), axis=-1, keepdims=True))
    return (rows - center) * lax.rsqrt(spread + 1e-05)

def apply_network(rows, first_layer, second_layer, third_layer, last_layer):
    highest = lax.Precision.HIGHEST
    hidden = jax.nn.silu(jnp.dot(rows, first_layer, precision=highest))
    hidden = jax.nn.silu(jnp.dot(hidden, second_layer, precision=highest))
    hidden = jax.nn.silu(jnp.dot(hidden, third_layer, precision=highest))
    return jnp.dot(hidden, last_layer, precision=highest)

def diffuse(state, diffusivity):
    padded = jnp.pad(state, ((0, 0), (0, 0), (1, 1), (1, 1)))
    neighbours = padded[:, :, 2:, 1:-1] + padded[:, :, :-2, 1:-1]
    neighbours = neighbours + padded[:, :, 1:-1, 2:] + padded[:, :, 1:-1, :-2]
    return state + diffusivity * (neighbours - 4.0 * state)

def reference(u_field, v_field, diffusivity, active_columns, regimes, first_layer, second_layer, third_layer, last_layer):
    state = jnp.stack([u_field, v_field])
    device = jnp.arange(ACT, dtype=jnp.int32) // A_DEV
    tile_pos = device // N_INF
    inf_pos = device % N_INF
    global_x = tile_pos * CX + active_columns // CY
    global_y = inf_pos * CY + active_columns % CY
    inputs = jnp.concatenate([u_field[:, global_x, global_y].T, v_field[:, global_x, global_y].T], axis=1)
    normed = standardize(inputs)
    owner = regimes[:, 0]
    order = jnp.argsort(owner, stable=True).astype(jnp.int32)
    sorted_owner = owner[order]
    labels = jnp.arange(EXPERTS, dtype=jnp.int32)
    starts = jnp.searchsorted(sorted_owner, labels, side='left').astype(jnp.int32)
    stops = jnp.searchsorted(sorted_owner, labels, side='right').astype(jnp.int32)
    slots = EXPERTS * CAP

    def per_regime(operands):
        start, stop, layer_one, layer_two, layer_three, layer_four = operands
        offsets = jnp.arange(slots, dtype=jnp.int32)
        positions = jnp.minimum(start + offsets, ACT - 1)
        picked = order[positions]
        result = apply_network(normed[picked], layer_one, layer_two, layer_three, layer_four)
        target = jnp.where(offsets < stop - start, picked, ACT).astype(jnp.int32)
        return (result, target)
    results, targets = lax.map(per_regime, (starts, stops, first_layer, second_layer, third_layer, last_layer))
    drag = jnp.zeros((ACT, 2 * LEV), jnp.float32).at[targets.reshape(-1)].set(results.reshape(-1, 2 * LEV), mode='drop')
    for step_index in range(PASSES):
        state = diffuse(state, diffusivity)
    tendency = drag.reshape(ACT, 2, LEV).transpose(1, 2, 0)
    state = state.at[:, :, global_x, global_y].add(tendency)
    return (state[0], state[1])
```

```python
import functools

import jax
import jax.numpy as jnp
from jax import lax
from jax.experimental import pallas as pl
from jax.experimental.pallas import tpu as pltpu
from jax.sharding import PartitionSpec as P

PASSES = 4


def exchange_kernel(count, me_axes, x_ref, o_ref, send_sem, recv_sem, own_sem):
    me = lax.axis_index("tile") * lax.axis_size("inf") + lax.axis_index("inf")

    def peer(step):
        return (me + step) % count

    barrier = pltpu.get_barrier_semaphore()

    def greet(step, carry):
        pl.semaphore_signal(barrier, inc=1, device_id=peer(step), device_id_type=pl.DeviceIdType.LOGICAL)
        return carry

    lax.fori_loop(1, count, greet, 0)
    own = pltpu.make_async_copy(x_ref.at[me], o_ref.at[me], own_sem)
    own.start()
    pl.semaphore_wait(barrier, count - 1)

    def send(step, carry):
        other = peer(step)
        pltpu.make_async_remote_copy(
            src_ref=x_ref.at[other],
            dst_ref=o_ref.at[me],
            send_sem=send_sem.at[step],
            recv_sem=recv_sem.at[step],
            device_id=other,
            device_id_type=pl.DeviceIdType.LOGICAL,
        ).start()
        return carry

    lax.fori_loop(1, count, send, 0)

    def finish(step, carry):
        source = (me - step + count) % count
        pltpu.make_async_remote_copy(
            src_ref=x_ref.at[peer(step)],
            dst_ref=o_ref.at[source],
            send_sem=send_sem.at[step],
            recv_sem=recv_sem.at[step],
            device_id=peer(step),
            device_id_type=pl.DeviceIdType.LOGICAL,
        ).wait()
        return carry

    lax.fori_loop(1, count, finish, 0)
    own.wait()


def exchange(x, number):
    count = x.shape[0]
    return pl.pallas_call(
        functools.partial(exchange_kernel, count, None),
        out_shape=jax.ShapeDtypeStruct(x.shape, x.dtype),
        in_specs=[pl.BlockSpec(memory_space=pltpu.VMEM)],
        out_specs=pl.BlockSpec(memory_space=pltpu.VMEM),
        scratch_shapes=[
            pltpu.SemaphoreType.DMA((count,)),
            pltpu.SemaphoreType.DMA((count,)),
            pltpu.SemaphoreType.DMA,
        ],
        compiler_params=pltpu.CompilerParams(
            collective_id=number, has_side_effects=True, vmem_limit_bytes=40 << 20
        ),
    )(x)


def with_halo(x, sides, width):
    for axis, dim in sides:
        count, length = (lax.axis_size(axis), x.shape[dim])
        up = [(i, (i + 1) % count) for i in range(count - 1)]
        down = [(j, i) for i, j in up]
        last = lax.slice_in_dim(x, length - width, length, axis=dim)
        first = lax.slice_in_dim(x, 0, width, axis=dim)
        before = lax.ppermute(last, axis, up)
        after = lax.ppermute(first, axis, down)
        x = jnp.concatenate([before, x, after], axis=dim)
    return x


def standardize(rows):
    center = jnp.mean(rows, axis=-1, keepdims=True)
    spread = jnp.mean(jnp.square(rows - center), axis=-1, keepdims=True)
    return (rows - center) * lax.rsqrt(spread + 1e-05)


def network_rows(rows, first_layer, second_layer, third_layer, last_layer):
    highest = lax.Precision.HIGHEST
    hidden = jax.nn.silu(jnp.dot(rows, first_layer, precision=highest))
    hidden = jax.nn.silu(jnp.dot(hidden, second_layer, precision=highest))
    hidden = jax.nn.silu(jnp.dot(hidden, third_layer, precision=highest))
    return jnp.dot(hidden, last_layer, precision=highest)


def single_pass(padded, center, coeffs):
    neighbours = padded[:, :, 2:, 1:-1] + padded[:, :, :-2, 1:-1]
    neighbours = neighbours + padded[:, :, 1:-1, 2:] + padded[:, :, 1:-1, :-2]
    return center + coeffs * (neighbours - 4.0 * center)


def body(
    u_field,
    v_field,
    diffusivity,
    active_columns,
    regimes,
    first_layer,
    second_layer,
    third_layer,
    last_layer,
):
    levels, width_x, width_y = u_field.shape
    features = 2 * levels
    cells = width_x * width_y
    active_count = active_columns.shape[0]
    devices_all = lax.axis_size(("tile", "inf"))
    capacity = 2 * active_count // devices_all
    slot_total = devices_all * capacity
    block_rows = min(512, active_count)
    block_count = active_count // block_rows
    state = jnp.stack([u_field, v_field])
    target = regimes[:, 0]
    labels = jnp.arange(devices_all, dtype=jnp.int32)
    one_hot = (
        (target[:, None] == labels[None, :])
        .astype(jnp.bfloat16)
        .reshape(block_count, block_rows, devices_all)
    )
    row_ids = jnp.arange(block_rows, dtype=jnp.int32)
    lower = (row_ids[:, None] > row_ids[None, :]).astype(jnp.bfloat16)

    def rank_step(counts, piece):
        earlier = jnp.dot(lower, piece, preferred_element_type=jnp.float32) + counts[None, :]
        wide_piece = piece.astype(jnp.float32)
        rank = jnp.sum(earlier * wide_piece, axis=1)
        return (counts + jnp.sum(wide_piece, axis=0), rank)

    _, ranks = lax.scan(rank_step, jnp.zeros((devices_all,), jnp.float32), one_hot)
    slot_index = target * capacity + ranks.reshape(-1).astype(jnp.int32)
    flat_state = state.reshape(features, cells)
    inputs = flat_state[:, active_columns].T
    outgoing = jnp.zeros((slot_total, features), jnp.float32).at[slot_index].set(inputs)
    block = exchange(outgoing.reshape(devices_all, capacity, features), 0)
    block_shape = block.shape
    rows = standardize(block.reshape(-1, features))
    result = network_rows(rows, first_layer[0], second_layer[0], third_layer[0], last_layer[0])
    answered = result.reshape(block_shape)
    returned = exchange(answered, 1)
    returned_rows = returned.reshape(slot_total, features)
    drag_rows = returned_rows[slot_index]
    for step_index in range(PASSES):
        padded = with_halo(state, (("tile", 2), ("inf", 3)), 1)
        state = single_pass(padded, state, diffusivity)
    final_flat = state.reshape(features, cells).at[:, active_columns].add(drag_rows.T)
    result = final_flat.reshape(2, levels, width_x, width_y)
    return (result[0], result[1])


def solution(mesh):
    in_specs = (
        P(None, "tile", "inf"),
        P(None, "tile", "inf"),
        P("tile", "inf"),
        P(("tile", "inf")),
        P(("tile", "inf"), None),
        P(("tile", "inf"), None, None),
        P(("tile", "inf"), None, None),
        P(("tile", "inf"), None, None),
        P(("tile", "inf"), None, None),
    )
    out_specs = (P(None, "tile", "inf"), P(None, "tile", "inf"))
    return jax.shard_map(body, mesh=mesh, in_specs=in_specs, out_specs=out_specs, check_vma=False)
```

```python
import functools

import jax
import jax.numpy as jnp
from jax import lax
from jax.experimental import pallas as pl
from jax.experimental.pallas import tpu as pltpu
from jax.sharding import PartitionSpec as P

PASSES = 4
LOGICAL = pl.DeviceIdType.LOGICAL
F32 = jnp.float32
BF16 = jnp.bfloat16

LEVELS = 64
FEATURES = 128
WX = 64
WY = 128
CAP = 32
DEVICES = 128
ACTIVE = 2048
ROWS_X = WX + 8
ROWS_Y = WY + 32
GROUP = 16
GROUPS = DEVICES // GROUP


def slot_kernel(regime_ref, column_ref, pick_ref, slot_ref):
    width = 256
    blocks = ACTIVE // width
    expert = lax.broadcasted_iota(jnp.int32, (DEVICES, width), 0)
    earlier = lax.broadcasted_iota(jnp.int32, (width, width), 0)
    later = lax.broadcasted_iota(jnp.int32, (width, width), 1)
    upper = (earlier < later).astype(BF16)
    place = lax.broadcasted_iota(jnp.int32, (CAP, width), 0)
    counts = jnp.zeros((DEVICES, 1), F32)
    pick_x = jnp.zeros((CAP, DEVICES), F32)
    pick_y = jnp.zeros((CAP, DEVICES), F32)
    for block in range(blocks):
        part = slice(block * width, (block + 1) * width)
        named = regime_ref[:, part]
        column = column_ref[:, part]
        hit = (expert == named).astype(F32)
        hit16 = hit.astype(BF16)
        before = jnp.dot(hit16, upper, preferred_element_type=F32) + counts
        rank = jnp.sum(before * hit, axis=0, keepdims=True).astype(jnp.int32)
        counts = counts + jnp.sum(hit, axis=1, keepdims=True)
        slot_ref[:, part] = named * CAP + rank
        chosen = (place == rank).astype(F32)
        x = (column // WY).astype(F32)
        y = (column % WY).astype(F32)
        dims = (((1,), (1,)), ((), ()))
        pick_x = pick_x + lax.dot_general((chosen * x).astype(BF16), hit16, dims, preferred_element_type=F32)
        pick_y = pick_y + lax.dot_general((chosen * y).astype(BF16), hit16, dims, preferred_element_type=F32)
    pick_ref[...] = (pick_x * WY + pick_y).astype(jnp.int32)


def find_slots(regimes, active_columns):
    vmem = pl.BlockSpec(memory_space=pltpu.VMEM)
    return pl.pallas_call(
        slot_kernel,
        out_shape=(
            jax.ShapeDtypeStruct((CAP, DEVICES), jnp.int32),
            jax.ShapeDtypeStruct((1, ACTIVE), jnp.int32),
        ),
        in_specs=[vmem, vmem],
        out_specs=(vmem, vmem),
    )(regimes.reshape(1, ACTIVE), active_columns.reshape(1, ACTIVE))


NEIGHBOURS = [(dx, dy) for dx in (-1, 0, 1) for dy in (-1, 0, 1) if (dx, dy) != (0, 0)]


def split(value):
    high = value.astype(BF16)
    return high, (value - high.astype(F32)).astype(BF16)


def product(rows, high_ref, low_ref):
    high, low = split(rows)
    total = jnp.dot(high, low_ref[...], preferred_element_type=F32)
    total = total + jnp.dot(low, high_ref[...], preferred_element_type=F32)
    return total + jnp.dot(high, high_ref[...], preferred_element_type=F32)


def silu(z):
    half = 0.5 * z
    return half + half * jnp.tanh(half)


def main_kernel(
    pick_ref,
    u_hbm,
    v_hbm,
    d_hbm,
    w1_hbm,
    w2_hbm,
    w3_hbm,
    w4_hbm,
    drag_ref,
    diffused_ref,
    fields,
    profiles,
    state,
    dext,
    dwide,
    send,
    recv,
    answer,
    w1,
    w2,
    w3,
    w4,
    w1h,
    w1l,
    w2h,
    w2l,
    w3h,
    w3l,
    w4h,
    w4l,
    load_sem,
    own_sem,
    weight_sem,
    halo_send,
    halo_recv,
    dhalo_send,
    dhalo_recv,
    out_send,
    out_recv,
    back_send,
    back_recv,
):
    tile = lax.axis_index("tile")
    inf = lax.axis_index("inf")
    me = tile * 8 + inf
    at_x, at_z = tile // 4, tile % 4
    at_y, at_c = inf // 2, inf % 2

    pieces = 4
    wide = WX // pieces
    loads = []
    for piece in range(pieces):
        part = pl.ds(piece * wide, wide)
        for which, source in enumerate((u_hbm, v_hbm)):
            loads.append(
                pltpu.make_async_copy(source.at[:, part, :], fields.at[which, :, part, :], load_sem.at[piece, which])
            )
    own_d = pltpu.make_async_copy(d_hbm, dext.at[1, pl.ds(8, WX), :], own_sem)
    weight_loads = [
        pltpu.make_async_copy(source.at[0], target, weight_sem.at[number])
        for number, (source, target) in enumerate(((w1_hbm, w1), (w2_hbm, w2), (w3_hbm, w3), (w4_hbm, w4)))
    ]
    for load in loads:
        load.start()
    own_d.start()
    for load in weight_loads:
        load.start()

    barrier = pltpu.get_barrier_semaphore()

    def greet(step, carry):
        other = me + step
        other = jnp.where(other >= DEVICES, other - DEVICES, other)
        pl.semaphore_signal(barrier, inc=1, device_id=other, device_id_type=LOGICAL)
        return carry

    lax.fori_loop(1, DEVICES, greet, 0)

    flat_fields = fields.reshape(2 * LEVELS * WX, WY)

    def turn(x, carry):
        block = flat_fields[pl.ds(x, FEATURES, stride=WX), :]
        block = block.T
        state[0, x + 4, 16 : 16 + WY, :] = block
        profiles[pl.ds(pl.multiple_of(x * WY, WY), WY), :] = block
        return carry

    for piece in range(pieces):
        loads[2 * piece].wait()
        loads[2 * piece + 1].wait()
        lax.fori_loop(piece * wide, (piece + 1) * wide, turn, 0)
    own_d.wait()

    @pl.when(tile == 0)
    def _():
        state[0, 0:4, 8 : 24 + WY, :] = jnp.zeros((4, WY + 16, FEATURES), F32)
        dext[:, 0:8, :] = jnp.zeros((3, 8, WY), F32)

    @pl.when(tile == 15)
    def _():
        state[0, WX + 4 : WX + 8, 8 : 24 + WY, :] = jnp.zeros((4, WY + 16, FEATURES), F32)
        dext[:, WX + 8 : WX + 16, :] = jnp.zeros((3, 8, WY), F32)

    @pl.when(inf == 0)
    def _():
        state[0, :, 8:16, :] = jnp.zeros((ROWS_X, 8, FEATURES), F32)
        dext[0, :, :] = jnp.zeros((WX + 16, WY), F32)

    @pl.when(inf == 7)
    def _():
        state[0, :, 16 + WY : 24 + WY, :] = jnp.zeros((ROWS_X, 8, FEATURES), F32)
        dext[2, :, :] = jnp.zeros((WX + 16, WY), F32)

    pl.semaphore_wait(barrier, DEVICES - 1)

    def halo(number):
        dx, dy = NEIGHBOURS[number]
        opposite = NEIGHBOURS.index((-dx, -dy))
        there_x, there_y = tile + dx, inf + dy
        exists = (there_x >= 0) & (there_x < 16) & (there_y >= 0) & (there_y < 8)
        comes_x, comes_y = tile - dx, inf - dy
        comes = (comes_x >= 0) & (comes_x < 16) & (comes_y >= 0) & (comes_y < 8)
        from_x = {1: pl.ds(WX, 4), -1: pl.ds(4, 4), 0: pl.ds(4, WX)}[dx]
        to_x = {1: pl.ds(0, 4), -1: pl.ds(WX + 4, 4), 0: pl.ds(4, WX)}[dx]
        from_y = {1: pl.ds(8 + WY, 8), -1: pl.ds(16, 8), 0: pl.ds(16, WY)}[dy]
        to_y = {1: pl.ds(8, 8), -1: pl.ds(16 + WY, 8), 0: pl.ds(16, WY)}[dy]
        from_d = {1: pl.ds(WX, 8), -1: pl.ds(8, 8), 0: pl.ds(8, WX)}[dx]
        to_d = {1: pl.ds(0, 8), -1: pl.ds(WX + 8, 8), 0: pl.ds(8, WX)}[dx]
        other = there_x * 8 + there_y
        profile = pltpu.make_async_remote_copy(
            src_ref=state.at[0, from_x, from_y, :],
            dst_ref=state.at[0, to_x, to_y, :],
            send_sem=halo_send.at[number],
            recv_sem=halo_recv.at[number],
            device_id=other,
            device_id_type=LOGICAL,
        )
        number_d = pltpu.make_async_remote_copy(
            src_ref=dext.at[1, from_d, :],
            dst_ref=dext.at[1 - dy, to_d, :],
            send_sem=dhalo_send.at[number],
            recv_sem=dhalo_recv.at[number],
            device_id=other,
            device_id_type=LOGICAL,
        )
        return exists, comes, profile, number_d

    for number in range(8):
        exists, _, profile, coefficient = halo(number)

        @pl.when(exists)
        def _():
            coefficient.start()
            profile.start()

    def target(turn_number, lane):
        x = (at_x + lane) % 4
        c = (at_c + lane // 4) % 2
        z = (at_z + lane + turn_number) % 4
        y = (at_y + lane + turn_number // 4) % 4
        return x * 32 + z * 8 + y * 2 + c

    def source(turn_number, lane):
        x = (at_x + 8 - lane) % 4
        c = (at_c + 2 - lane // 4) % 2
        z = (at_z + 24 - lane - turn_number) % 4
        y = (at_y + 12 - lane - turn_number // 4) % 4
        return x * 32 + z * 8 + y * 2 + c

    def away(step, other, group):
        return pltpu.make_async_remote_copy(
            src_ref=send.at[step],
            dst_ref=recv.at[step],
            send_sem=out_send,
            recv_sem=out_recv.at[group],
            device_id=other,
            device_id_type=LOGICAL,
        )

    def back(step, other):
        return pltpu.make_async_remote_copy(
            src_ref=answer.at[step],
            dst_ref=drag_ref.at[me],
            send_sem=back_send,
            recv_sem=back_recv,
            device_id=other,
            device_id_type=LOGICAL,
        )

    def dispatch(turn_number, carry):
        for lane in range(8):
            step = turn_number * 8 + lane
            other = target(turn_number, lane)
            for k in range(CAP):
                row = pick_ref[k, other]
                send[step, k : k + 1, :] = profiles[pl.ds(row, 1), :]
            if lane == 0:

                @pl.when(turn_number > 0)
                def _():
                    away(step, other, turn_number // 2).start()
            else:
                away(step, other, turn_number // 2).start()
        return carry

    lax.fori_loop(0, DEVICES // 8, dispatch, 0)
    recv[0] = send[0]

    for load in weight_loads:
        load.wait()
    for whole, high_ref, low_ref in ((w1, w1h, w1l), (w2, w2h, w2l), (w3, w3h, w3l), (w4, w4h, w4l)):
        high, low = split(whole[...])
        high_ref[...] = high
        low_ref[...] = low

    for number in range(8):
        exists, comes, profile, coefficient = halo(number)

        @pl.when(comes)
        def _():
            coefficient.wait_recv()
            profile.wait_recv()

        @pl.when(exists)
        def _():
            coefficient.wait_send()
            profile.wait_send()

    lane = lax.broadcasted_iota(jnp.int32, (WX + 16, WY), 1)
    left = pltpu.roll(dext[0], 8, 1)
    right = pltpu.roll(dext[2], 8, 1)
    sides = jnp.where(lane < 8, left, right)
    sides = jnp.concatenate([sides, jnp.zeros((WY - WX - 16, WY), F32)], axis=0).T[0:16, :]

    def widen(x, carry):
        row = dext[1, pl.ds(x + 4, 1), :]
        dwide[x, 16 : 16 + WY, :] = jnp.broadcast_to(row, (WY, FEATURES)).T
        column = pltpu.roll(sides, WY - 4 - x, 1)[:, 0:1]
        column = jnp.broadcast_to(column, (16, FEATURES))
        dwide[x, 8:16, :] = column[0:8]
        dwide[x, 16 + WY : 24 + WY, :] = column[8:16]
        return carry

    lax.fori_loop(1, ROWS_X - 1, widen, 0)

    def diffuse(number):
        held, following = number % 2, 1 - number % 2
        last = number == PASSES - 1
        first = number + 1
        count = (ROWS_X - 2 * first) // 2
        cuts = [(16 + 64 * cut, 64) for cut in range(2)] if last else [(8 + 48 * cut, 48) for cut in range(3)]

        def rows(step, carry):
            x = first + 2 * step
            for start, size in cuts:
                middle = [state[held, x - 1 + k, start : start + size, :] for k in range(4)]
                for k in range(2):
                    q = middle[k + 1]
                    near = middle[k] + middle[k + 2]
                    near = near + state[held, x + k, start - 1 : start + size - 1, :]
                    near = near + state[held, x + k, start + 1 : start + size + 1, :]
                    new = q + dwide[x + k, start : start + size, :] * (near - 4.0 * q)
                    if last:
                        diffused_ref[x + k - 4, start - 16 : start - 16 + size, :] = new
                    else:
                        state[following, x + k, start : start + size, :] = new
            return carry

        lax.fori_loop(0, count, rows, 0)

    def network(group, carry):
        rows = recv[pl.ds(group * GROUP, GROUP)].reshape(GROUP * CAP, FEATURES)
        center = jnp.mean(rows, axis=-1, keepdims=True)
        shifted = rows - center
        spread = jnp.mean(shifted * shifted, axis=-1, keepdims=True)
        rows = shifted * lax.rsqrt(spread + 1e-05)
        hidden = silu(product(rows, w1h, w1l))
        hidden = silu(product(hidden, w2h, w2l))
        hidden = silu(product(hidden, w3h, w3l))
        result = product(hidden, w4h, w4l)
        answer[pl.ds(group * GROUP, GROUP)] = result.reshape(GROUP, CAP, FEATURES)
        for part in range(2):
            for lane in range(8):
                turn_number = group * 2 + part
                step = turn_number * 8 + lane
                other = source(turn_number, lane)
                if part == 0 and lane == 0:

                    @pl.when(group > 0)
                    def _():
                        back(step, other).start()
                else:
                    back(step, other).start()
        return carry

    def arrived(first, count, group):
        pltpu.make_async_remote_copy(
            src_ref=recv.at[pl.ds(first, count)],
            dst_ref=recv.at[pl.ds(first, count)],
            send_sem=out_send,
            recv_sem=out_recv.at[group],
            device_id=me,
            device_id_type=LOGICAL,
        ).wait_recv()

    def arrived_network(group, carry):
        arrived(group * GROUP, GROUP, group)
        return network(group, carry)

    for number in range(2):
        diffuse(number)
    arrived(1, GROUP - 1, 0)
    network(0, 0)
    drag_ref[me] = answer[0]
    lax.fori_loop(1, 4, arrived_network, 0)
    for number in range(2, PASSES):
        diffuse(number)
    lax.fori_loop(4, GROUPS, arrived_network, 0)

    others = DEVICES - 1
    pltpu.make_async_remote_copy(
        src_ref=answer.at[pl.ds(0, others)],
        dst_ref=drag_ref.at[pl.ds(0, others)],
        send_sem=back_send,
        recv_sem=back_recv,
        device_id=me,
        device_id_type=LOGICAL,
    ).wait()
    pltpu.make_async_remote_copy(
        src_ref=send.at[pl.ds(0, others)],
        dst_ref=recv.at[pl.ds(0, others)],
        send_sem=out_send,
        recv_sem=out_recv.at[0],
        device_id=me,
        device_id_type=LOGICAL,
    ).wait_send()


def drag_and_diffusion(pick, u_field, v_field, diffusivity, layers):
    vmem = pl.BlockSpec(memory_space=pltpu.VMEM)
    smem = pl.BlockSpec(memory_space=pltpu.SMEM)
    hbm = pl.BlockSpec(memory_space=pl.ANY)
    shapes = [layer.shape[1:] for layer in layers]
    halves = [pltpu.VMEM(shape, BF16) for shape in shapes for _ in range(2)]
    dma = pltpu.SemaphoreType.DMA
    return pl.pallas_call(
        main_kernel,
        out_shape=(
            jax.ShapeDtypeStruct((DEVICES, CAP, FEATURES), F32),
            jax.ShapeDtypeStruct((WX, WY, FEATURES), F32),
        ),
        in_specs=[smem] + [hbm] * 7,
        out_specs=(vmem, vmem),
        scratch_shapes=[
            pltpu.VMEM((2, LEVELS, WX, WY), F32),
            pltpu.VMEM((WX * WY, FEATURES), F32),
            pltpu.VMEM((2, ROWS_X, ROWS_Y, FEATURES), F32),
            pltpu.VMEM((3, WX + 16, WY), F32),
            pltpu.VMEM((ROWS_X, ROWS_Y, FEATURES), F32),
            pltpu.VMEM((DEVICES, CAP, FEATURES), F32),
            pltpu.VMEM((DEVICES, CAP, FEATURES), F32),
            pltpu.VMEM((DEVICES, CAP, FEATURES), F32),
            *[pltpu.VMEM(shape, F32) for shape in shapes],
            *halves,
            dma((4, 2)),
            dma,
            dma((4,)),
            dma((8,)),
            dma((8,)),
            dma((8,)),
            dma((8,)),
            dma,
            dma((GROUPS,)),
            dma,
            dma,
        ],
        compiler_params=pltpu.CompilerParams(
            collective_id=0, has_side_effects=True, vmem_limit_bytes=50 << 20
        ),
    )(pick, u_field, v_field, diffusivity, *layers)


def place_kernel(column_ref, slot_ref, drag_ref, diffused_ref, u_hbm, v_hbm, dense, staged, out_sem):
    def clear(x, carry):
        dense[pl.ds(x * WY, WY), :] = jnp.zeros((WY, FEATURES), F32)
        return carry

    lax.fori_loop(0, WX, clear, 0)
    drags = drag_ref.reshape(DEVICES * CAP, FEATURES)

    def place(step, carry):
        for k in range(16):
            row = step * 16 + k
            dense[pl.ds(column_ref[row], 1), :] = drags[pl.ds(slot_ref[0, row], 1), :]
        return carry

    lax.fori_loop(0, ACTIVE // 16, place, 0)
    flat = staged.reshape(2 * LEVELS * WX, WY)

    def turn(x, carry):
        block = dense[pl.ds(x * WY, WY), :] + diffused_ref[x]
        flat[pl.ds(x, FEATURES, stride=WX), :] = block.T
        return carry

    pieces = 4
    wide = WX // pieces
    copies = []
    for piece in range(pieces):
        lax.fori_loop(piece * wide, (piece + 1) * wide, turn, 0)
        part = pl.ds(piece * wide, wide)
        for which, target in enumerate((u_hbm, v_hbm)):
            copy = pltpu.make_async_copy(staged.at[which, :, part, :], target.at[:, part, :], out_sem.at[piece, which])
            copy.start()
            copies.append(copy)
    for copy in copies:
        copy.wait()


def place_drag(active_columns, slots, drag, diffused):
    vmem = pl.BlockSpec(memory_space=pltpu.VMEM)
    smem = pl.BlockSpec(memory_space=pltpu.SMEM)
    hbm = pl.BlockSpec(memory_space=pl.ANY)
    shape = jax.ShapeDtypeStruct((LEVELS, WX, WY), F32)
    return pl.pallas_call(
        place_kernel,
        out_shape=(shape, shape),
        in_specs=[smem, smem, vmem, vmem],
        out_specs=(hbm, hbm),
        scratch_shapes=[
            pltpu.VMEM((WX * WY, FEATURES), F32),
            pltpu.VMEM((2, LEVELS, WX, WY), F32),
            pltpu.SemaphoreType.DMA((4, 2)),
        ],
        compiler_params=pltpu.CompilerParams(vmem_limit_bytes=30 << 20),
    )(active_columns, slots, drag, diffused)


def body(
    u_field,
    v_field,
    diffusivity,
    active_columns,
    regimes,
    first_layer,
    second_layer,
    third_layer,
    last_layer,
):
    pick, slots = find_slots(regimes, active_columns)
    layers = (first_layer, second_layer, third_layer, last_layer)
    drag, diffused = drag_and_diffusion(pick, u_field, v_field, diffusivity, layers)
    return place_drag(active_columns, slots, drag, diffused)


def solution(mesh):
    in_specs = (
        P(None, "tile", "inf"),
        P(None, "tile", "inf"),
        P("tile", "inf"),
        P(("tile", "inf")),
        P(("tile", "inf"), None),
        P(("tile", "inf"), None, None),
        P(("tile", "inf"), None, None),
        P(("tile", "inf"), None, None),
        P(("tile", "inf"), None, None),
    )
    out_specs = (P(None, "tile", "inf"), P(None, "tile", "inf"))
    return jax.shard_map(body, mesh=mesh, in_specs=in_specs, out_specs=out_specs, check_vma=False)
```

```python
import functools

import jax
import jax.numpy as jnp
from jax import lax
from jax.experimental import pallas as pl
from jax.experimental.pallas import tpu as pltpu
from jax.sharding import PartitionSpec as P

PASSES = 4
LOGICAL = pl.DeviceIdType.LOGICAL
F32 = jnp.float32
BF16 = jnp.bfloat16

LEVELS = 64
FEATURES = 128
WX = 64
WY = 128
CAP = 32
DEVICES = 128
ACTIVE = 2048
ROWS_X = WX + 8
ROWS_Y = WY + 32
GROUP = 16
GROUPS = DEVICES // GROUP


def slot_kernel(regime_ref, column_ref, pick_ref, slot_ref):
    width = 256
    blocks = ACTIVE // width
    expert = lax.broadcasted_iota(jnp.int32, (DEVICES, width), 0)
    earlier = lax.broadcasted_iota(jnp.int32, (width, width), 0)
    later = lax.broadcasted_iota(jnp.int32, (width, width), 1)
    upper = (earlier < later).astype(BF16)
    place = lax.broadcasted_iota(jnp.int32, (CAP, width), 0)
    counts = jnp.zeros((DEVICES, 1), F32)
    pick_x = jnp.zeros((CAP, DEVICES), F32)
    pick_y = jnp.zeros((CAP, DEVICES), F32)
    for block in range(blocks):
        part = slice(block * width, (block + 1) * width)
        named = regime_ref[:, part]
        column = column_ref[:, part]
        hit = (expert == named).astype(F32)
        hit16 = hit.astype(BF16)
        before = jnp.dot(hit16, upper, preferred_element_type=F32) + counts
        rank = jnp.sum(before * hit, axis=0, keepdims=True).astype(jnp.int32)
        counts = counts + jnp.sum(hit, axis=1, keepdims=True)
        slot_ref[:, part] = named * CAP + rank
        chosen = (place == rank).astype(F32)
        x = (column // WY).astype(F32)
        y = (column % WY).astype(F32)
        dims = (((1,), (1,)), ((), ()))
        pick_x = pick_x + lax.dot_general((chosen * x).astype(BF16), hit16, dims, preferred_element_type=F32)
        pick_y = pick_y + lax.dot_general((chosen * y).astype(BF16), hit16, dims, preferred_element_type=F32)
    pick_ref[...] = (pick_x * WY + pick_y).astype(jnp.int32)


def find_slots(regimes, active_columns):
    vmem = pl.BlockSpec(memory_space=pltpu.VMEM)
    return pl.pallas_call(
        slot_kernel,
        out_shape=(
            jax.ShapeDtypeStruct((CAP, DEVICES), jnp.int32),
            jax.ShapeDtypeStruct((1, ACTIVE), jnp.int32),
        ),
        in_specs=[vmem, vmem],
        out_specs=(vmem, vmem),
    )(regimes.reshape(1, ACTIVE), active_columns.reshape(1, ACTIVE))


NEIGHBOURS = [(dx, dy) for dx in (-1, 0, 1) for dy in (-1, 0, 1) if (dx, dy) != (0, 0)]


def split(value):
    high = value.astype(BF16)
    return high, (value - high.astype(F32)).astype(BF16)


def product(rows, high_ref, low_ref):
    high, low = split(rows)
    total = jnp.dot(high, low_ref[...], preferred_element_type=F32)
    total = total + jnp.dot(low, high_ref[...], preferred_element_type=F32)
    return total + jnp.dot(high, high_ref[...], preferred_element_type=F32)


def silu(z):
    half = 0.5 * z
    return half + half * jnp.tanh(half)


def main_kernel(
    pick_ref,
    u_hbm,
    v_hbm,
    d_hbm,
    w1_hbm,
    w2_hbm,
    w3_hbm,
    w4_hbm,
    drag_ref,
    diffused_hbm,
    fields,
    profiles,
    state,
    dext,
    sides_ref,
    dwide,
    send,
    recv,
    answer,
    w1,
    w2,
    w3,
    w4,
    w1h,
    w1l,
    w2h,
    w2l,
    w3h,
    w3l,
    w4h,
    w4l,
    load_sem,
    own_sem,
    weight_sem,
    halo_send,
    halo_recv,
    dhalo_send,
    dhalo_recv,
    out_send,
    out_recv,
    back_send,
    back_recv,
    diffused_sem,
):
    tile = lax.axis_index("tile")
    inf = lax.axis_index("inf")
    me = tile * 8 + inf
    at_x, at_z = tile // 4, tile % 4
    at_y, at_c = inf // 2, inf % 2

    pieces = 4
    wide = WX // pieces
    loads = []
    for piece in range(pieces):
        part = pl.ds(piece * wide, wide)
        for which, source in enumerate((u_hbm, v_hbm)):
            loads.append(
                pltpu.make_async_copy(source.at[:, part, :], fields.at[which, :, part, :], load_sem.at[piece, which])
            )
    own_d = pltpu.make_async_copy(d_hbm, dext.at[1, pl.ds(8, WX), :], own_sem)
    weight_loads = [
        pltpu.make_async_copy(source.at[0], target, weight_sem.at[number])
        for number, (source, target) in enumerate(((w1_hbm, w1), (w2_hbm, w2), (w3_hbm, w3), (w4_hbm, w4)))
    ]
    for load in loads:
        load.start()
    own_d.start()
    for load in weight_loads:
        load.start()

    barrier = pltpu.get_barrier_semaphore()

    def greet(step):
        other = me + step
        other = jnp.where(other >= DEVICES, other - DEVICES, other)
        pl.semaphore_signal(barrier, inc=1, device_id=other, device_id_type=LOGICAL)

    flat_fields = fields.reshape(2 * LEVELS * WX, WY)

    def turn(step, carry):
        for k in range(4):
            x = 4 * step + k
            if k < 3:
                greet(2 * x + 1)
                greet(2 * x + 2)
            block = flat_fields[pl.ds(x, FEATURES, stride=WX), :].T
            state[0, x + 4, 16 : 16 + WY, :] = block
            profiles[pl.ds(pl.multiple_of(x * WY, WY), WY), :] = block
        x = 4 * step + 3

        greet(2 * x + 1)

        @pl.when(step < WX // 4 - 1)
        def _():
            greet(2 * x + 2)

        return carry

    for piece in range(pieces):
        loads[2 * piece].wait()
        loads[2 * piece + 1].wait()
        lax.fori_loop(piece * wide // 4, (piece + 1) * wide // 4, turn, 0)
    own_d.wait()

    @pl.when(tile == 0)
    def _():
        state[0, 0:4, 8 : 24 + WY, :] = jnp.zeros((4, WY + 16, FEATURES), F32)
        dext[:, 0:8, :] = jnp.zeros((3, 8, WY), F32)

    @pl.when(tile == 15)
    def _():
        state[0, WX + 4 : WX + 8, 8 : 24 + WY, :] = jnp.zeros((4, WY + 16, FEATURES), F32)
        dext[:, WX + 8 : WX + 16, :] = jnp.zeros((3, 8, WY), F32)

    @pl.when(inf == 0)
    def _():
        state[0, :, 8:16, :] = jnp.zeros((ROWS_X, 8, FEATURES), F32)
        dext[0, :, :] = jnp.zeros((WX + 16, WY), F32)

    @pl.when(inf == 7)
    def _():
        state[0, :, 16 + WY : 24 + WY, :] = jnp.zeros((ROWS_X, 8, FEATURES), F32)
        dext[2, :, :] = jnp.zeros((WX + 16, WY), F32)

    pl.semaphore_wait(barrier, DEVICES - 1)

    def halo(number):
        dx, dy = NEIGHBOURS[number]
        opposite = NEIGHBOURS.index((-dx, -dy))
        there_x, there_y = tile + dx, inf + dy
        exists = (there_x >= 0) & (there_x < 16) & (there_y >= 0) & (there_y < 8)
        comes_x, comes_y = tile - dx, inf - dy
        comes = (comes_x >= 0) & (comes_x < 16) & (comes_y >= 0) & (comes_y < 8)
        from_x = {1: pl.ds(WX, 4), -1: pl.ds(4, 4), 0: pl.ds(4, WX)}[dx]
        to_x = {1: pl.ds(0, 4), -1: pl.ds(WX + 4, 4), 0: pl.ds(4, WX)}[dx]
        from_y = {1: pl.ds(8 + WY, 8), -1: pl.ds(16, 8), 0: pl.ds(16, WY)}[dy]
        to_y = {1: pl.ds(8, 8), -1: pl.ds(16 + WY, 8), 0: pl.ds(16, WY)}[dy]
        from_d = {1: pl.ds(WX, 8), -1: pl.ds(8, 8), 0: pl.ds(8, WX)}[dx]
        to_d = {1: pl.ds(0, 8), -1: pl.ds(WX + 8, 8), 0: pl.ds(8, WX)}[dx]
        other = there_x * 8 + there_y
        profile = pltpu.make_async_remote_copy(
            src_ref=state.at[0, from_x, from_y, :],
            dst_ref=state.at[0, to_x, to_y, :],
            send_sem=halo_send.at[number],
            recv_sem=halo_recv.at[number],
            device_id=other,
            device_id_type=LOGICAL,
        )
        number_d = pltpu.make_async_remote_copy(
            src_ref=dext.at[1, from_d, :],
            dst_ref=dext.at[1 - dy, to_d, :],
            send_sem=dhalo_send.at[number],
            recv_sem=dhalo_recv.at[number],
            device_id=other,
            device_id_type=LOGICAL,
        )
        return exists, comes, profile, number_d

    for number in range(8):
        exists, _, profile, coefficient = halo(number)

        @pl.when(exists)
        def _():
            coefficient.start()
            profile.start()

    def target(turn_number, lane):
        x = (at_x + lane) % 4
        c = (at_c + lane // 4) % 2
        z = (at_z + lane + turn_number) % 4
        y = (at_y + lane + turn_number // 4) % 4
        return x * 32 + z * 8 + y * 2 + c

    def source(turn_number, lane):
        x = (at_x + 8 - lane) % 4
        c = (at_c + 2 - lane // 4) % 2
        z = (at_z + 24 - lane - turn_number) % 4
        y = (at_y + 12 - lane - turn_number // 4) % 4
        return x * 32 + z * 8 + y * 2 + c

    def away(step, other, group):
        return pltpu.make_async_remote_copy(
            src_ref=send.at[step],
            dst_ref=recv.at[step],
            send_sem=out_send,
            recv_sem=out_recv.at[group],
            device_id=other,
            device_id_type=LOGICAL,
        )

    def back(step, other):
        return pltpu.make_async_remote_copy(
            src_ref=answer.at[step],
            dst_ref=drag_ref.at[me],
            send_sem=back_send,
            recv_sem=back_recv,
            device_id=other,
            device_id_type=LOGICAL,
        )

    def dispatch(turn_number, carry):
        for lane in range(8):
            step = turn_number * 8 + lane
            other = target(turn_number, lane)
            for k in range(CAP):
                row = pick_ref[k, other]
                send[step, k : k + 1, :] = profiles[pl.ds(row, 1), :]
            if lane == 0:

                @pl.when(turn_number > 0)
                def _():
                    away(step, other, turn_number // 2).start()
            else:
                away(step, other, turn_number // 2).start()
        return carry

    lax.fori_loop(0, DEVICES // 8, dispatch, 0)
    recv[0] = send[0]

    for load in weight_loads:
        load.wait()
    for whole, high_ref, low_ref in ((w1, w1h, w1l), (w2, w2h, w2l), (w3, w3h, w3l), (w4, w4h, w4l)):
        high, low = split(whole[...])
        high_ref[...] = high
        low_ref[...] = low

    def receive_halo():
        for number in range(8):
            exists, comes, profile, coefficient = halo(number)

            @pl.when(comes)
            def _():
                coefficient.wait_recv()
                profile.wait_recv()

            @pl.when(exists)
            def _():
                coefficient.wait_send()
                profile.wait_send()

        lane = lax.broadcasted_iota(jnp.int32, (WX + 16, WY), 1)
        left = pltpu.roll(dext[0], 8, 1)
        right = pltpu.roll(dext[2], 8, 1)
        sides = jnp.where(lane < 8, left, right)
        sides_ref[...] = jnp.concatenate([sides, jnp.zeros((WY - WX - 16, WY), F32)], axis=0).T[0:16, :]

    def widen(step, carry):
        for k in range(4):
            x = 4 * step + k
            row = dext[1, pl.ds(x + 4, 1), :]
            dwide[x, 16 : 16 + WY, :] = jnp.broadcast_to(row, (WY, FEATURES)).T
            column = pltpu.roll(sides_ref[...], WY - 4 - x, 1)[:, 0:1]
            column = jnp.broadcast_to(column, (16, FEATURES))
            dwide[x, 8:16, :] = column[0:8]
            dwide[x, 16 + WY : 24 + WY, :] = column[8:16]
        return carry

    def diffuse(number):
        held, following = number % 2, 1 - number % 2
        last = number == PASSES - 1
        first = number + 1
        count = (ROWS_X - 2 * first) // 2
        cuts = [(16 + 64 * cut, 64) for cut in range(2)] if last else [(8 + 48 * cut, 48) for cut in range(3)]

        def rows(step, carry):
            x = first + 2 * step
            for start, size in cuts:
                middle = [state[held, x - 1 + k, start : start + size, :] for k in range(4)]
                for k in range(2):
                    q = middle[k + 1]
                    near = middle[k] + middle[k + 2]
                    near = near + state[held, x + k, start - 1 : start + size - 1, :]
                    near = near + state[held, x + k, start + 1 : start + size + 1, :]
                    new = q + dwide[x + k, start : start + size, :] * (near - 4.0 * q)
                    if last:
                        at = pl.multiple_of((x + k - 4) * WY, WY) + start - 16
                        profiles[pl.ds(pl.multiple_of(at, 8), size), :] = new
                    else:
                        state[following, x + k, start : start + size, :] = new
            return carry

        lax.fori_loop(0, count, rows, 0)

    def network(group, carry):
        rows = recv[pl.ds(group * GROUP, GROUP)].reshape(GROUP * CAP, FEATURES)
        center = jnp.mean(rows, axis=-1, keepdims=True)
        shifted = rows - center
        spread = jnp.mean(shifted * shifted, axis=-1, keepdims=True)
        rows = shifted * lax.rsqrt(spread + 1e-05)
        hidden = silu(product(rows, w1h, w1l))
        hidden = silu(product(hidden, w2h, w2l))
        hidden = silu(product(hidden, w3h, w3l))
        result = product(hidden, w4h, w4l)
        answer[pl.ds(group * GROUP, GROUP)] = result.reshape(GROUP, CAP, FEATURES)
        for part in range(2):
            for lane in range(8):
                turn_number = group * 2 + part
                step = turn_number * 8 + lane
                other = source(turn_number, lane)
                if part == 0 and lane == 0:

                    @pl.when(group > 0)
                    def _():
                        back(step, other).start()
                else:
                    back(step, other).start()
        return carry

    def arrived(first, count, group):
        pltpu.make_async_remote_copy(
            src_ref=recv.at[pl.ds(first, count)],
            dst_ref=recv.at[pl.ds(first, count)],
            send_sem=out_send,
            recv_sem=out_recv.at[group],
            device_id=me,
            device_id_type=LOGICAL,
        ).wait_recv()

    def arrived_network(group, carry):
        @pl.when(group == 0)
        def _():
            arrived(1, GROUP - 1, 0)

        @pl.when(group > 0)
        def _():
            arrived(group * GROUP, GROUP, group)

        network(group, carry)

        @pl.when(group == 1)
        def _():
            receive_halo()
            lax.fori_loop(0, ROWS_X // 8, widen, 0)

        @pl.when(group == 3)
        def _():
            lax.fori_loop(ROWS_X // 8, ROWS_X // 4, widen, 0)

        @pl.when(group == 4)
        def _():
            diffuse(0)

        @pl.when(group == 5)
        def _():
            diffuse(1)

        return carry

    lax.fori_loop(0, GROUPS, arrived_network, 0)
    drag_ref[me] = answer[0]
    diffuse(2)
    diffuse(3)
    diffused = pltpu.make_async_copy(profiles, diffused_hbm, diffused_sem)
    diffused.start()

    others = DEVICES - 1
    pltpu.make_async_remote_copy(
        src_ref=answer.at[pl.ds(0, others)],
        dst_ref=drag_ref.at[pl.ds(0, others)],
        send_sem=back_send,
        recv_sem=back_recv,
        device_id=me,
        device_id_type=LOGICAL,
    ).wait()
    pltpu.make_async_remote_copy(
        src_ref=send.at[pl.ds(0, others)],
        dst_ref=recv.at[pl.ds(0, others)],
        send_sem=out_send,
        recv_sem=out_recv.at[0],
        device_id=me,
        device_id_type=LOGICAL,
    ).wait_send()
    diffused.wait()


def drag_and_diffusion(pick, u_field, v_field, diffusivity, layers):
    vmem = pl.BlockSpec(memory_space=pltpu.VMEM)
    smem = pl.BlockSpec(memory_space=pltpu.SMEM)
    hbm = pl.BlockSpec(memory_space=pltpu.HBM)
    shapes = [layer.shape[1:] for layer in layers]
    halves = [pltpu.VMEM(shape, BF16) for shape in shapes for _ in range(2)]
    dma = pltpu.SemaphoreType.DMA
    return pl.pallas_call(
        main_kernel,
        out_shape=(
            jax.ShapeDtypeStruct((DEVICES, CAP, FEATURES), F32),
            jax.ShapeDtypeStruct((WX * WY, FEATURES), F32),
        ),
        in_specs=[smem] + [hbm] * 7,
        out_specs=(vmem, hbm),
        scratch_shapes=[
            pltpu.VMEM((2, LEVELS, WX, WY), F32),
            pltpu.VMEM((WX * WY, FEATURES), F32),
            pltpu.VMEM((2, ROWS_X, ROWS_Y, FEATURES), F32),
            pltpu.VMEM((3, WX + 16, WY), F32),
            pltpu.VMEM((16, WY), F32),
            pltpu.VMEM((ROWS_X, ROWS_Y, FEATURES), F32),
            pltpu.VMEM((DEVICES, CAP, FEATURES), F32),
            pltpu.VMEM((DEVICES, CAP, FEATURES), F32),
            pltpu.VMEM((DEVICES, CAP, FEATURES), F32),
            *[pltpu.VMEM(shape, F32) for shape in shapes],
            *halves,
            dma((4, 2)),
            dma,
            dma((4,)),
            dma((8,)),
            dma((8,)),
            dma((8,)),
            dma((8,)),
            dma,
            dma((GROUPS,)),
            dma,
            dma,
            dma,
        ],
        compiler_params=pltpu.CompilerParams(
            collective_id=0, has_side_effects=True, vmem_limit_bytes=59840 << 10
        ),
    )(pick, u_field, v_field, diffusivity, *layers)


def place_kernel(
    column_ref, slot_ref, drag_ref, diffused_hbm, u_hbm, v_hbm, dense, diffused, staged, in_sem, out_sem
):
    pieces = 4
    wide = WX // pieces
    loads = []
    for piece in range(pieces):
        part = pl.ds(piece * wide * WY, wide * WY)
        load = pltpu.make_async_copy(diffused_hbm.at[part], diffused.at[part], in_sem.at[piece])
        load.start()
        loads.append(load)

    def clear(x, carry):
        dense[pl.ds(pl.multiple_of(x * WY, WY), WY), :] = jnp.zeros((WY, FEATURES), F32)
        return carry

    lax.fori_loop(0, WX, clear, 0)
    drags = drag_ref.reshape(DEVICES * CAP, FEATURES)

    def place(step, carry):
        rows = [drags[pl.ds(slot_ref[0, step * 16 + k], 1), :] for k in range(16)]
        for k in range(16):
            dense[pl.ds(column_ref[step * 16 + k], 1), :] = rows[k]
        return carry

    lax.fori_loop(0, ACTIVE // 16, place, 0)
    flat = staged.reshape(2 * LEVELS * WX, WY)

    def turn(step, carry):
        for k in range(4):
            x = 4 * step + k
            part = pl.ds(pl.multiple_of(x * WY, WY), WY)
            block = dense[part, :] + diffused[part, :]
            flat[pl.ds(x, FEATURES, stride=WX), :] = block.T
        return carry

    copies = []
    for piece in range(pieces):
        loads[piece].wait()
        lax.fori_loop(piece * wide // 4, (piece + 1) * wide // 4, turn, 0)
        part = pl.ds(piece * wide, wide)
        for which, target in enumerate((u_hbm, v_hbm)):
            copy = pltpu.make_async_copy(staged.at[which, :, part, :], target.at[:, part, :], out_sem.at[piece, which])
            copy.start()
            copies.append(copy)
    for copy in copies:
        copy.wait()


def place_drag(active_columns, slots, drag, diffused):
    vmem = pl.BlockSpec(memory_space=pltpu.VMEM)
    smem = pl.BlockSpec(memory_space=pltpu.SMEM)
    hbm = pl.BlockSpec(memory_space=pltpu.HBM)
    shape = jax.ShapeDtypeStruct((LEVELS, WX, WY), F32)
    return pl.pallas_call(
        place_kernel,
        out_shape=(shape, shape),
        in_specs=[smem, smem, vmem, hbm],
        out_specs=(hbm, hbm),
        scratch_shapes=[
            pltpu.VMEM((WX * WY, FEATURES), F32),
            pltpu.VMEM((WX * WY, FEATURES), F32),
            pltpu.VMEM((2, LEVELS, WX, WY), F32),
            pltpu.SemaphoreType.DMA((4,)),
            pltpu.SemaphoreType.DMA((4, 2)),
        ],
        compiler_params=pltpu.CompilerParams(vmem_limit_bytes=59840 << 10),
    )(active_columns, slots, drag, diffused)


def body(
    u_field,
    v_field,
    diffusivity,
    active_columns,
    regimes,
    first_layer,
    second_layer,
    third_layer,
    last_layer,
):
    pick, slots = find_slots(regimes, active_columns)
    layers = (first_layer, second_layer, third_layer, last_layer)
    drag, diffused = drag_and_diffusion(pick, u_field, v_field, diffusivity, layers)
    return place_drag(active_columns, slots, drag, diffused)


def solution(mesh):
    in_specs = (
        P(None, "tile", "inf"),
        P(None, "tile", "inf"),
        P("tile", "inf"),
        P(("tile", "inf")),
        P(("tile", "inf"), None),
        P(("tile", "inf"), None, None),
        P(("tile", "inf"), None, None),
        P(("tile", "inf"), None, None),
        P(("tile", "inf"), None, None),
    )
    out_specs = (P(None, "tile", "inf"), P(None, "tile", "inf"))
    return jax.shard_map(body, mesh=mesh, in_specs=in_specs, out_specs=out_specs, check_vma=False)
```

```python
import functools

import jax
import jax.numpy as jnp
from jax import lax
from jax.experimental import pallas as pl
from jax.experimental.pallas import tpu as pltpu
from jax.sharding import PartitionSpec as P

PASSES = 4
LOGICAL = pl.DeviceIdType.LOGICAL
F32 = jnp.float32
BF16 = jnp.bfloat16

LEVELS = 64
FEATURES = 128
WX = 64
WY = 128
CAP = 32
DEVICES = 128
ACTIVE = 2048
ROWS_X = WX + 8
ROWS_Y = WY + 32
GROUP = 16
PADDED = WX + 8
GROUPS = DEVICES // GROUP


def find_slots(regime_ref, column_ref, pick_ref, slot_ref):
    width = 256
    blocks = ACTIVE // width
    expert = lax.broadcasted_iota(jnp.int32, (DEVICES, width), 0)
    earlier = lax.broadcasted_iota(jnp.int32, (width, width), 0)
    later = lax.broadcasted_iota(jnp.int32, (width, width), 1)
    upper = (earlier < later).astype(BF16)
    place = lax.broadcasted_iota(jnp.int32, (CAP, width), 0)
    counts = jnp.zeros((DEVICES, 1), F32)
    pick_x = jnp.zeros((CAP, DEVICES), F32)
    pick_y = jnp.zeros((CAP, DEVICES), F32)
    for block in range(blocks):
        part = slice(block * width, (block + 1) * width)
        named = regime_ref[:, part]
        column = column_ref[:, part]
        hit = (expert == named).astype(F32)
        hit16 = hit.astype(BF16)
        before = jnp.dot(hit16, upper, preferred_element_type=F32) + counts
        rank = jnp.sum(before * hit, axis=0, keepdims=True).astype(jnp.int32)
        counts = counts + jnp.sum(hit, axis=1, keepdims=True)
        slot_ref[:, part] = named * CAP + rank
        chosen = (place == rank).astype(F32)
        x = (column // WY).astype(F32)
        y = (column % WY).astype(F32)
        dims = (((1,), (1,)), ((), ()))
        pick_x = pick_x + lax.dot_general((chosen * x).astype(BF16), hit16, dims, preferred_element_type=F32)
        pick_y = pick_y + lax.dot_general((chosen * y).astype(BF16), hit16, dims, preferred_element_type=F32)
    pick_ref[...] = jnp.clip((pick_x * WY + pick_y).astype(jnp.int32), 0, WX * WY - 1)


NEIGHBOURS = [(dx, dy) for dx in (-1, 0, 1) for dy in (-1, 0, 1) if (dx, dy) != (0, 0)]


def split(value):
    high = value.astype(BF16)
    return high, (value - high.astype(F32)).astype(BF16)


def product(rows, high_ref, low_ref):
    high, low = split(rows)
    total = jnp.dot(high, low_ref[...], preferred_element_type=F32)
    total = total + jnp.dot(low, high_ref[...], preferred_element_type=F32)
    return total + jnp.dot(high, high_ref[...], preferred_element_type=F32)


def silu(z):
    half = 0.5 * z
    return half + half * jnp.tanh(half)


def main_kernel(
    regime_ref,
    column_ref,
    u_hbm,
    v_hbm,
    d_hbm,
    w1_hbm,
    w2_hbm,
    w3_hbm,
    w4_hbm,
    drag_ref,
    diffused_hbm,
    slot_ref,
    pick_vmem,
    pick_ref,
    fields,
    profiles,
    state,
    dext,
    sides_ref,
    dwide,
    send,
    recv,
    answer,
    w1,
    w2,
    w3,
    w4,
    w1h,
    w1l,
    w2h,
    w2l,
    w3h,
    w3l,
    w4h,
    w4l,
    load_sem,
    own_sem,
    weight_sem,
    halo_send,
    halo_recv,
    dhalo_send,
    dhalo_recv,
    out_send,
    out_recv,
    back_send,
    back_recv,
    diffused_sem,
    pick_sem,
):
    tile = lax.axis_index("tile")
    inf = lax.axis_index("inf")
    me = tile * 8 + inf
    at_x, at_z = tile // 4, tile % 4
    at_y, at_c = inf // 2, inf % 2

    pieces = 4
    wide = WX // pieces
    loads = []
    for piece in range(pieces):
        part = pl.ds(piece * wide, wide)
        for which, source in enumerate((u_hbm, v_hbm)):
            loads.append(
                pltpu.make_async_copy(source.at[:, part, :], fields.at[which, :, part, :], load_sem.at[piece, which])
            )
    own_d = pltpu.make_async_copy(d_hbm, dext.at[1, pl.ds(8, WX), :], own_sem)
    weight_loads = [
        pltpu.make_async_copy(source.at[0], target, weight_sem.at[number])
        for number, (source, target) in enumerate(((w1_hbm, w1), (w2_hbm, w2), (w3_hbm, w3), (w4_hbm, w4)))
    ]
    for load in loads:
        load.start()
    own_d.start()
    for load in weight_loads:
        load.start()

    barrier = pltpu.get_barrier_semaphore()

    def greet(step, carry):
        other = me + step
        other = jnp.where(other >= DEVICES, other - DEVICES, other)
        pl.semaphore_signal(barrier, inc=1, device_id=other, device_id_type=LOGICAL)
        return carry

    lax.fori_loop(1, DEVICES, greet, 0)

    find_slots(regime_ref, column_ref, pick_vmem, slot_ref)
    picks = pltpu.make_async_copy(pick_vmem, pick_ref, pick_sem)
    picks.start()

    flat_fields = fields.reshape(2 * LEVELS * PADDED, WY)

    def turn(step, carry):
        for k in range(4):
            x = 4 * step + k
            block = flat_fields[pl.ds(x, FEATURES, stride=PADDED), :].T
            state[0, x + 4, 16 : 16 + WY, :] = block
            profiles[pl.ds(pl.multiple_of(x * WY, WY), WY), :] = block
        return carry

    for piece in range(pieces):
        loads[2 * piece].wait()
        loads[2 * piece + 1].wait()
        lax.fori_loop(piece * wide // 4, (piece + 1) * wide // 4, turn, 0)
    own_d.wait()
    picks.wait()

    @pl.when(tile == 0)
    def _():
        state[0, 0:4, 8 : 24 + WY, :] = jnp.zeros((4, WY + 16, FEATURES), F32)
        dext[:, 0:8, :] = jnp.zeros((3, 8, WY), F32)

    @pl.when(tile == 15)
    def _():
        state[0, WX + 4 : WX + 8, 8 : 24 + WY, :] = jnp.zeros((4, WY + 16, FEATURES), F32)
        dext[:, WX + 8 : WX + 16, :] = jnp.zeros((3, 8, WY), F32)

    @pl.when(inf == 0)
    def _():
        state[0, :, 8:16, :] = jnp.zeros((ROWS_X, 8, FEATURES), F32)
        dext[0, :, :] = jnp.zeros((WX + 16, WY), F32)

    @pl.when(inf == 7)
    def _():
        state[0, :, 16 + WY : 24 + WY, :] = jnp.zeros((ROWS_X, 8, FEATURES), F32)
        dext[2, :, :] = jnp.zeros((WX + 16, WY), F32)

    pl.semaphore_wait(barrier, DEVICES - 1)

    def halo(number):
        dx, dy = NEIGHBOURS[number]
        opposite = NEIGHBOURS.index((-dx, -dy))
        there_x, there_y = tile + dx, inf + dy
        exists = (there_x >= 0) & (there_x < 16) & (there_y >= 0) & (there_y < 8)
        comes_x, comes_y = tile - dx, inf - dy
        comes = (comes_x >= 0) & (comes_x < 16) & (comes_y >= 0) & (comes_y < 8)
        from_x = {1: pl.ds(WX, 4), -1: pl.ds(4, 4), 0: pl.ds(4, WX)}[dx]
        to_x = {1: pl.ds(0, 4), -1: pl.ds(WX + 4, 4), 0: pl.ds(4, WX)}[dx]
        from_y = {1: pl.ds(8 + WY, 8), -1: pl.ds(16, 8), 0: pl.ds(16, WY)}[dy]
        to_y = {1: pl.ds(8, 8), -1: pl.ds(16 + WY, 8), 0: pl.ds(16, WY)}[dy]
        from_d = {1: pl.ds(WX, 8), -1: pl.ds(8, 8), 0: pl.ds(8, WX)}[dx]
        to_d = {1: pl.ds(0, 8), -1: pl.ds(WX + 8, 8), 0: pl.ds(8, WX)}[dx]
        other = there_x * 8 + there_y
        profile = pltpu.make_async_remote_copy(
            src_ref=state.at[0, from_x, from_y, :],
            dst_ref=state.at[0, to_x, to_y, :],
            send_sem=halo_send.at[number],
            recv_sem=halo_recv.at[number],
            device_id=other,
            device_id_type=LOGICAL,
        )
        number_d = pltpu.make_async_remote_copy(
            src_ref=dext.at[1, from_d, :],
            dst_ref=dext.at[1 - dy, to_d, :],
            send_sem=dhalo_send.at[number],
            recv_sem=dhalo_recv.at[number],
            device_id=other,
            device_id_type=LOGICAL,
        )
        return exists, comes, profile, number_d

    for number in range(8):
        exists, _, profile, coefficient = halo(number)

        @pl.when(exists)
        def _():
            coefficient.start()
            profile.start()

    def target(turn_number, lane):
        x = (at_x + lane) % 4
        c = (at_c + lane // 4) % 2
        z = (at_z + lane + turn_number) % 4
        y = (at_y + lane + turn_number // 4) % 4
        return x * 32 + z * 8 + y * 2 + c

    def source(turn_number, lane):
        x = (at_x + 8 - lane) % 4
        c = (at_c + 2 - lane // 4) % 2
        z = (at_z + 24 - lane - turn_number) % 4
        y = (at_y + 12 - lane - turn_number // 4) % 4
        return x * 32 + z * 8 + y * 2 + c

    def away(step, other, group):
        return pltpu.make_async_remote_copy(
            src_ref=send.at[step],
            dst_ref=recv.at[step],
            send_sem=out_send,
            recv_sem=out_recv.at[group],
            device_id=other,
            device_id_type=LOGICAL,
        )

    def back(step, other):
        return pltpu.make_async_remote_copy(
            src_ref=answer.at[step],
            dst_ref=drag_ref.at[me],
            send_sem=back_send,
            recv_sem=back_recv,
            device_id=other,
            device_id_type=LOGICAL,
        )

    def dispatch(turn_number, carry):
        for lane in range(8):
            step = turn_number * 8 + lane
            other = target(turn_number, lane)
            for k in range(CAP):
                row = pick_ref[k, other]
                send[step, k : k + 1, :] = profiles[pl.ds(row, 1), :]
            if lane == 0:

                @pl.when(turn_number > 0)
                def _():
                    away(step, other, turn_number // 2).start()
            else:
                away(step, other, turn_number // 2).start()
        return carry

    lax.fori_loop(0, DEVICES // 8, dispatch, 0)
    recv[0] = send[0]

    for load in weight_loads:
        load.wait()
    for whole, high_ref, low_ref in ((w1, w1h, w1l), (w2, w2h, w2l), (w3, w3h, w3l), (w4, w4h, w4l)):
        high, low = split(whole[...])
        high_ref[...] = high
        low_ref[...] = low

    def receive_halo():
        for number in range(8):
            exists, comes, profile, coefficient = halo(number)

            @pl.when(comes)
            def _():
                coefficient.wait_recv()
                profile.wait_recv()

            @pl.when(exists)
            def _():
                coefficient.wait_send()
                profile.wait_send()

        lane = lax.broadcasted_iota(jnp.int32, (WX + 16, WY), 1)
        left = pltpu.roll(dext[0], 8, 1)
        right = pltpu.roll(dext[2], 8, 1)
        sides = jnp.where(lane < 8, left, right)
        sides_ref[...] = jnp.concatenate([sides, jnp.zeros((WY - WX - 16, WY), F32)], axis=0).T[0:16, :]

    def widen(step, carry):
        for k in range(4):
            x = 4 * step + k
            row = dext[1, pl.ds(x + 4, 1), :]
            dwide[x, 16 : 16 + WY, :] = jnp.broadcast_to(row, (WY, FEATURES)).T
            column = pltpu.roll(sides_ref[...], WY - 4 - x, 1)[:, 0:1]
            column = jnp.broadcast_to(column, (16, FEATURES))
            dwide[x, 8:16, :] = column[0:8]
            dwide[x, 16 + WY : 24 + WY, :] = column[8:16]
        return carry

    def diffuse(number):
        held, following = number % 2, 1 - number % 2
        last = number == PASSES - 1
        first = number + 1
        count = (ROWS_X - 2 * first) // 2
        cuts = [(16 + 64 * cut, 64) for cut in range(2)] if last else [(8 + 48 * cut, 48) for cut in range(3)]

        def rows(step, carry):
            x = first + 2 * step
            for start, size in cuts:
                middle = [state[held, x - 1 + k, start : start + size, :] for k in range(4)]
                for k in range(2):
                    q = middle[k + 1]
                    near = middle[k] + middle[k + 2]
                    near = near + state[held, x + k, start - 1 : start + size - 1, :]
                    near = near + state[held, x + k, start + 1 : start + size + 1, :]
                    new = q + dwide[x + k, start : start + size, :] * (near - 4.0 * q)
                    if last:
                        at = pl.multiple_of((x + k - 4) * WY, WY) + start - 16
                        profiles[pl.ds(pl.multiple_of(at, 8), size), :] = new
                    else:
                        state[following, x + k, start : start + size, :] = new
            return carry

        lax.fori_loop(0, count, rows, 0)

    def network(group, carry):
        rows = recv[pl.ds(group * GROUP, GROUP)].reshape(GROUP * CAP, FEATURES)
        center = jnp.mean(rows, axis=-1, keepdims=True)
        shifted = rows - center
        spread = jnp.mean(shifted * shifted, axis=-1, keepdims=True)
        rows = shifted * lax.rsqrt(spread + 1e-05)
        hidden = silu(product(rows, w1h, w1l))
        hidden = silu(product(hidden, w2h, w2l))
        hidden = silu(product(hidden, w3h, w3l))
        result = product(hidden, w4h, w4l)
        answer[pl.ds(group * GROUP, GROUP)] = result.reshape(GROUP, CAP, FEATURES)
        for part in range(2):
            for lane in range(8):
                turn_number = group * 2 + part
                step = turn_number * 8 + lane
                other = source(turn_number, lane)
                if part == 0 and lane == 0:

                    @pl.when(group > 0)
                    def _():
                        back(step, other).start()
                else:
                    back(step, other).start()
        return carry

    def arrived(first, count, group):
        pltpu.make_async_remote_copy(
            src_ref=recv.at[pl.ds(first, count)],
            dst_ref=recv.at[pl.ds(first, count)],
            send_sem=out_send,
            recv_sem=out_recv.at[group],
            device_id=me,
            device_id_type=LOGICAL,
        ).wait_recv()

    def arrived_network(group, carry):
        @pl.when(group == 0)
        def _():
            arrived(1, GROUP - 1, 0)

        @pl.when(group > 0)
        def _():
            arrived(group * GROUP, GROUP, group)

        network(group, carry)

        return carry

    lax.fori_loop(0, GROUPS, arrived_network, 0)
    drag_ref[me] = answer[0]
    receive_halo()
    lax.fori_loop(0, ROWS_X // 4, widen, 0)
    diffuse(0)
    diffuse(1)
    diffuse(2)
    diffuse(3)
    diffused = pltpu.make_async_copy(profiles, diffused_hbm, diffused_sem)
    diffused.start()

    others = DEVICES - 1
    pltpu.make_async_remote_copy(
        src_ref=answer.at[pl.ds(0, others)],
        dst_ref=drag_ref.at[pl.ds(0, others)],
        send_sem=back_send,
        recv_sem=back_recv,
        device_id=me,
        device_id_type=LOGICAL,
    ).wait()
    pltpu.make_async_remote_copy(
        src_ref=send.at[pl.ds(0, others)],
        dst_ref=recv.at[pl.ds(0, others)],
        send_sem=out_send,
        recv_sem=out_recv.at[0],
        device_id=me,
        device_id_type=LOGICAL,
    ).wait_send()
    diffused.wait()


def drag_and_diffusion(regimes, active_columns, u_field, v_field, diffusivity, layers):
    vmem = pl.BlockSpec(memory_space=pltpu.VMEM)
    hbm = pl.BlockSpec(memory_space=pltpu.HBM)
    shapes = [layer.shape[1:] for layer in layers]
    halves = [pltpu.VMEM(shape, BF16) for shape in shapes for _ in range(2)]
    dma = pltpu.SemaphoreType.DMA
    return pl.pallas_call(
        main_kernel,
        out_shape=(
            jax.ShapeDtypeStruct((DEVICES, CAP, FEATURES), F32),
            jax.ShapeDtypeStruct((WX * WY, FEATURES), F32),
            jax.ShapeDtypeStruct((1, ACTIVE), jnp.int32),
        ),
        in_specs=[vmem, vmem] + [hbm] * 7,
        out_specs=(vmem, hbm, vmem),
        scratch_shapes=[
            pltpu.VMEM((CAP, DEVICES), jnp.int32),
            pltpu.SMEM((CAP, DEVICES), jnp.int32),
            pltpu.VMEM((2, LEVELS, PADDED, WY), F32),
            pltpu.VMEM((WX * WY, FEATURES), F32),
            pltpu.VMEM((2, ROWS_X, ROWS_Y, FEATURES), F32),
            pltpu.VMEM((3, WX + 16, WY), F32),
            pltpu.VMEM((16, WY), F32),
            pltpu.VMEM((ROWS_X, ROWS_Y, FEATURES), F32),
            pltpu.VMEM((DEVICES, CAP, FEATURES), F32),
            pltpu.VMEM((DEVICES, CAP, FEATURES), F32),
            pltpu.VMEM((DEVICES, CAP, FEATURES), F32),
            *[pltpu.VMEM(shape, F32) for shape in shapes],
            *halves,
            dma((4, 2)),
            dma,
            dma((4,)),
            dma((8,)),
            dma((8,)),
            dma((8,)),
            dma((8,)),
            dma,
            dma((GROUPS,)),
            dma,
            dma,
            dma,
            dma,
        ],
        compiler_params=pltpu.CompilerParams(
            collective_id=0, has_side_effects=True, vmem_limit_bytes=59840 << 10
        ),
    )(regimes.reshape(1, ACTIVE), active_columns.reshape(1, ACTIVE), u_field, v_field, diffusivity, *layers)


def place_kernel(
    column_ref, slot_ref, drag_ref, diffused_hbm, u_hbm, v_hbm, dense, diffused, staged, in_sem, out_sem
):
    pieces = 4
    wide = WX // pieces
    loads = []
    for piece in range(pieces):
        part = pl.ds(piece * wide * WY, wide * WY)
        load = pltpu.make_async_copy(diffused_hbm.at[part], diffused.at[part], in_sem.at[piece])
        load.start()
        loads.append(load)

    def clear(x, carry):
        dense[pl.ds(pl.multiple_of(x * WY, WY), WY), :] = jnp.zeros((WY, FEATURES), F32)
        return carry

    lax.fori_loop(0, WX, clear, 0)
    drags = drag_ref.reshape(DEVICES * CAP, FEATURES)

    def place(step, carry):
        rows = [drags[pl.ds(slot_ref[0, step * 16 + k], 1), :] for k in range(16)]
        for k in range(16):
            dense[pl.ds(column_ref[step * 16 + k], 1), :] = rows[k]
        return carry

    lax.fori_loop(0, ACTIVE // 16, place, 0)
    flat = staged.reshape(2 * LEVELS * PADDED, WY)

    def turn(step, carry):
        for k in range(4):
            x = 4 * step + k
            part = pl.ds(pl.multiple_of(x * WY, WY), WY)
            block = dense[part, :] + diffused[part, :]
            flat[pl.ds(x, FEATURES, stride=PADDED), :] = block.T
        return carry

    copies = []
    for piece in range(pieces):
        loads[piece].wait()
        lax.fori_loop(piece * wide // 4, (piece + 1) * wide // 4, turn, 0)
        part = pl.ds(piece * wide, wide)
        for which, target in enumerate((u_hbm, v_hbm)):
            copy = pltpu.make_async_copy(staged.at[which, :, part, :], target.at[:, part, :], out_sem.at[piece, which])
            copy.start()
            copies.append(copy)
    for copy in copies:
        copy.wait()


def place_drag(active_columns, slots, drag, diffused):
    vmem = pl.BlockSpec(memory_space=pltpu.VMEM)
    smem = pl.BlockSpec(memory_space=pltpu.SMEM)
    hbm = pl.BlockSpec(memory_space=pltpu.HBM)
    shape = jax.ShapeDtypeStruct((LEVELS, WX, WY), F32)
    return pl.pallas_call(
        place_kernel,
        out_shape=(shape, shape),
        in_specs=[smem, smem, vmem, hbm],
        out_specs=(hbm, hbm),
        scratch_shapes=[
            pltpu.VMEM((WX * WY, FEATURES), F32),
            pltpu.VMEM((WX * WY, FEATURES), F32),
            pltpu.VMEM((2, LEVELS, PADDED, WY), F32),
            pltpu.SemaphoreType.DMA((4,)),
            pltpu.SemaphoreType.DMA((4, 2)),
        ],
        compiler_params=pltpu.CompilerParams(vmem_limit_bytes=59840 << 10),
    )(active_columns, slots, drag, diffused)


def body(
    u_field,
    v_field,
    diffusivity,
    active_columns,
    regimes,
    first_layer,
    second_layer,
    third_layer,
    last_layer,
):
    layers = (first_layer, second_layer, third_layer, last_layer)
    drag, diffused, slots = drag_and_diffusion(regimes, active_columns, u_field, v_field, diffusivity, layers)
    return place_drag(active_columns, slots, drag, diffused)


def solution(mesh):
    in_specs = (
        P(None, "tile", "inf"),
        P(None, "tile", "inf"),
        P("tile", "inf"),
        P(("tile", "inf")),
        P(("tile", "inf"), None),
        P(("tile", "inf"), None, None),
        P(("tile", "inf"), None, None),
        P(("tile", "inf"), None, None),
        P(("tile", "inf"), None, None),
    )
    out_specs = (P(None, "tile", "inf"), P(None, "tile", "inf"))
    return jax.shard_map(body, mesh=mesh, in_specs=in_specs, out_specs=out_specs, check_vma=False)
```

```python
import functools

import jax
import jax.numpy as jnp
from jax import lax
from jax.experimental import pallas as pl
from jax.experimental.pallas import tpu as pltpu
from jax.sharding import PartitionSpec as P

PASSES = 4
LOGICAL = pl.DeviceIdType.LOGICAL
F32 = jnp.float32
BF16 = jnp.bfloat16

LEVELS = 64
FEATURES = 128
WX = 64
WY = 128
CAP = 32
DEVICES = 128
ACTIVE = 2048
ROWS_X = WX + 8
ROWS_Y = WY + 32
GROUP = 32
PADDED = WX + 8
GROUPS = DEVICES // GROUP
TURNS = GROUP // 8


def find_slots(regime_ref, column_ref, pick_ref, slot_ref):
    width = 256
    blocks = ACTIVE // width
    expert = lax.broadcasted_iota(jnp.int32, (DEVICES, width), 0)
    earlier = lax.broadcasted_iota(jnp.int32, (width, width), 0)
    later = lax.broadcasted_iota(jnp.int32, (width, width), 1)
    upper = (earlier < later).astype(BF16)
    place = lax.broadcasted_iota(jnp.int32, (CAP, width), 0)
    counts = jnp.zeros((DEVICES, 1), F32)
    pick_x = jnp.zeros((CAP, DEVICES), F32)
    pick_y = jnp.zeros((CAP, DEVICES), F32)
    for block in range(blocks):
        part = slice(block * width, (block + 1) * width)
        named = regime_ref[:, part]
        column = column_ref[:, part]
        hit = (expert == named).astype(F32)
        hit16 = hit.astype(BF16)
        before = jnp.dot(hit16, upper, preferred_element_type=F32) + counts
        rank = jnp.sum(before * hit, axis=0, keepdims=True).astype(jnp.int32)
        counts = counts + jnp.sum(hit, axis=1, keepdims=True)
        slot_ref[:, part] = named * CAP + rank
        chosen = (place == rank).astype(F32)
        x = (column // WY).astype(F32)
        y = (column % WY).astype(F32)
        dims = (((1,), (1,)), ((), ()))
        pick_x = pick_x + lax.dot_general((chosen * x).astype(BF16), hit16, dims, preferred_element_type=F32)
        pick_y = pick_y + lax.dot_general((chosen * y).astype(BF16), hit16, dims, preferred_element_type=F32)
    pick_ref[...] = jnp.clip((pick_x * WY + pick_y).astype(jnp.int32), 0, WX * WY - 1)


NEIGHBOURS = [(dx, dy) for dx in (-1, 0, 1) for dy in (-1, 0, 1) if (dx, dy) != (0, 0)]


def split(value):
    high = value.astype(BF16)
    return high, (value - high.astype(F32)).astype(BF16)


def product(rows, high_ref, low_ref):
    high, low = split(rows)
    total = jnp.dot(high, low_ref[...], preferred_element_type=F32)
    total = total + jnp.dot(low, high_ref[...], preferred_element_type=F32)
    return total + jnp.dot(high, high_ref[...], preferred_element_type=F32)


def silu(z):
    half = 0.5 * z
    return half + half * jnp.tanh(half)


def main_kernel(
    regime_ref,
    column_ref,
    u_hbm,
    v_hbm,
    d_hbm,
    w1_hbm,
    w2_hbm,
    w3_hbm,
    w4_hbm,
    drag_hbm,
    diffused_hbm,
    slot_ref,
    pick_vmem,
    pick_ref,
    fields,
    profiles,
    state,
    dext,
    sides_ref,
    dwide,
    send,
    recv,
    answer,
    w1,
    w2,
    w3,
    w4,
    w1h,
    w1l,
    w2h,
    w2l,
    w3h,
    w3l,
    w4h,
    w4l,
    load_sem,
    own_sem,
    weight_sem,
    halo_send,
    halo_recv,
    dhalo_send,
    dhalo_recv,
    out_send,
    out_recv,
    back_send,
    back_recv,
    diffused_sem,
    pick_sem,
):
    tile = lax.axis_index("tile")
    inf = lax.axis_index("inf")
    me = tile * 8 + inf
    at_x, at_z = tile // 4, tile % 4
    at_y, at_c = inf // 2, inf % 2

    pieces = 4
    wide = WX // pieces
    loads = []
    for piece in range(pieces):
        part = pl.ds(piece * wide, wide)
        for which, source in enumerate((u_hbm, v_hbm)):
            loads.append(
                pltpu.make_async_copy(source.at[:, part, :], fields.at[which, :, part, :], load_sem.at[piece, which])
            )
    own_d = pltpu.make_async_copy(d_hbm, dext.at[1, pl.ds(8, WX), :], own_sem)
    weight_loads = [
        pltpu.make_async_copy(source.at[0], target, weight_sem.at[number])
        for number, (source, target) in enumerate(((w1_hbm, w1), (w2_hbm, w2), (w3_hbm, w3), (w4_hbm, w4)))
    ]
    for load in loads:
        load.start()
    own_d.start()
    for load in weight_loads:
        load.start()

    barrier = pltpu.get_barrier_semaphore()

    def greet(step, carry):
        other = me + step
        other = jnp.where(other >= DEVICES, other - DEVICES, other)
        pl.semaphore_signal(barrier, inc=1, device_id=other, device_id_type=LOGICAL)
        return carry

    lax.fori_loop(1, DEVICES, greet, 0)

    find_slots(regime_ref, column_ref, pick_vmem, slot_ref)
    picks = pltpu.make_async_copy(pick_vmem, pick_ref, pick_sem)
    picks.start()

    flat_fields = fields.reshape(2 * LEVELS * PADDED, WY)

    def turn(step, carry):
        for k in range(4):
            x = 4 * step + k
            block = flat_fields[pl.ds(x, FEATURES, stride=PADDED), :].T
            state[0, x + 4, 16 : 16 + WY, :] = block
            profiles[pl.ds(pl.multiple_of(x * WY, WY), WY), :] = block
        return carry

    for piece in range(pieces):
        loads[2 * piece].wait()
        loads[2 * piece + 1].wait()
        lax.fori_loop(piece * wide // 4, (piece + 1) * wide // 4, turn, 0)
    own_d.wait()
    picks.wait()

    @pl.when(tile == 0)
    def _():
        state[0, 0:4, 8 : 24 + WY, :] = jnp.zeros((4, WY + 16, FEATURES), F32)
        dext[:, 0:8, :] = jnp.zeros((3, 8, WY), F32)

    @pl.when(tile == 15)
    def _():
        state[0, WX + 4 : WX + 8, 8 : 24 + WY, :] = jnp.zeros((4, WY + 16, FEATURES), F32)
        dext[:, WX + 8 : WX + 16, :] = jnp.zeros((3, 8, WY), F32)

    @pl.when(inf == 0)
    def _():
        state[0, :, 8:16, :] = jnp.zeros((ROWS_X, 8, FEATURES), F32)
        dext[0, :, :] = jnp.zeros((WX + 16, WY), F32)

    @pl.when(inf == 7)
    def _():
        state[0, :, 16 + WY : 24 + WY, :] = jnp.zeros((ROWS_X, 8, FEATURES), F32)
        dext[2, :, :] = jnp.zeros((WX + 16, WY), F32)

    pl.semaphore_wait(barrier, DEVICES - 1)

    def halo(number):
        dx, dy = NEIGHBOURS[number]
        opposite = NEIGHBOURS.index((-dx, -dy))
        there_x, there_y = tile + dx, inf + dy
        exists = (there_x >= 0) & (there_x < 16) & (there_y >= 0) & (there_y < 8)
        comes_x, comes_y = tile - dx, inf - dy
        comes = (comes_x >= 0) & (comes_x < 16) & (comes_y >= 0) & (comes_y < 8)
        from_x = {1: pl.ds(WX, 4), -1: pl.ds(4, 4), 0: pl.ds(4, WX)}[dx]
        to_x = {1: pl.ds(0, 4), -1: pl.ds(WX + 4, 4), 0: pl.ds(4, WX)}[dx]
        from_y = {1: pl.ds(8 + WY, 8), -1: pl.ds(16, 8), 0: pl.ds(16, WY)}[dy]
        to_y = {1: pl.ds(8, 8), -1: pl.ds(16 + WY, 8), 0: pl.ds(16, WY)}[dy]
        from_d = {1: pl.ds(WX, 8), -1: pl.ds(8, 8), 0: pl.ds(8, WX)}[dx]
        to_d = {1: pl.ds(0, 8), -1: pl.ds(WX + 8, 8), 0: pl.ds(8, WX)}[dx]
        other = there_x * 8 + there_y
        profile = pltpu.make_async_remote_copy(
            src_ref=state.at[0, from_x, from_y, :],
            dst_ref=state.at[0, to_x, to_y, :],
            send_sem=halo_send.at[number],
            recv_sem=halo_recv.at[number],
            device_id=other,
            device_id_type=LOGICAL,
        )
        number_d = pltpu.make_async_remote_copy(
            src_ref=dext.at[1, from_d, :],
            dst_ref=dext.at[1 - dy, to_d, :],
            send_sem=dhalo_send.at[number],
            recv_sem=dhalo_recv.at[number],
            device_id=other,
            device_id_type=LOGICAL,
        )
        return exists, comes, profile, number_d

    for number in range(8):
        exists, _, profile, coefficient = halo(number)

        @pl.when(exists)
        def _():
            coefficient.start()
            profile.start()

    def target(turn_number, lane):
        x = (at_x + lane) % 4
        c = (at_c + lane // 4) % 2
        z = (at_z + lane + turn_number) % 4
        y = (at_y + lane + turn_number // 4) % 4
        return x * 32 + z * 8 + y * 2 + c

    def source(turn_number, lane):
        x = (at_x + 8 - lane) % 4
        c = (at_c + 2 - lane // 4) % 2
        z = (at_z + 24 - lane - turn_number) % 4
        y = (at_y + 12 - lane - turn_number // 4) % 4
        return x * 32 + z * 8 + y * 2 + c

    def away(step, other, group):
        return pltpu.make_async_remote_copy(
            src_ref=send.at[step],
            dst_ref=recv.at[step],
            send_sem=out_send,
            recv_sem=out_recv.at[group],
            device_id=other,
            device_id_type=LOGICAL,
        )

    def back(step, other):
        return pltpu.make_async_remote_copy(
            src_ref=answer.at[step],
            dst_ref=drag_hbm.at[me],
            send_sem=back_send,
            recv_sem=back_recv,
            device_id=other,
            device_id_type=LOGICAL,
        )

    def dispatch(turn_number, carry):
        for lane in range(8):
            step = turn_number * 8 + lane
            other = target(turn_number, lane)
            for k in range(CAP):
                row = pick_ref[k, other]
                send[step, k : k + 1, :] = profiles[pl.ds(row, 1), :]
            if lane == 0:

                @pl.when(turn_number > 0)
                def _():
                    away(step, other, turn_number // TURNS).start()
            else:
                away(step, other, turn_number // TURNS).start()
        return carry

    lax.fori_loop(0, DEVICES // 8, dispatch, 0)
    recv[0] = send[0]

    for load in weight_loads:
        load.wait()
    for whole, high_ref, low_ref in ((w1, w1h, w1l), (w2, w2h, w2l), (w3, w3h, w3l), (w4, w4h, w4l)):
        high, low = split(whole[...])
        high_ref[...] = high
        low_ref[...] = low

    def receive_halo():
        for number in range(8):
            exists, comes, profile, coefficient = halo(number)

            @pl.when(comes)
            def _():
                coefficient.wait_recv()
                profile.wait_recv()

            @pl.when(exists)
            def _():
                coefficient.wait_send()
                profile.wait_send()

        lane = lax.broadcasted_iota(jnp.int32, (WX + 16, WY), 1)
        left = pltpu.roll(dext[0], 8, 1)
        right = pltpu.roll(dext[2], 8, 1)
        sides = jnp.where(lane < 8, left, right)
        sides_ref[...] = jnp.concatenate([sides, jnp.zeros((WY - WX - 16, WY), F32)], axis=0).T[0:16, :]

    def widen(step, carry):
        for k in range(4):
            x = 4 * step + k
            row = dext[1, pl.ds(x + 4, 1), :]
            dwide[x, 16 : 16 + WY, :] = jnp.broadcast_to(row, (WY, FEATURES)).T
            column = pltpu.roll(sides_ref[...], WY - 4 - x, 1)[:, 0:1]
            column = jnp.broadcast_to(column, (16, FEATURES))
            dwide[x, 8:16, :] = column[0:8]
            dwide[x, 16 + WY : 24 + WY, :] = column[8:16]
        return carry

    def diffuse(number):
        held, following = number % 2, 1 - number % 2
        last = number == PASSES - 1
        first = number + 1
        count = (ROWS_X - 2 * first) // 2
        cuts = [(16 + 64 * cut, 64) for cut in range(2)] if last else [(8 + 48 * cut, 48) for cut in range(3)]

        def rows(step, carry):
            x = first + 2 * step
            for start, size in cuts:
                middle = [state[held, x - 1 + k, start : start + size, :] for k in range(4)]
                for k in range(2):
                    q = middle[k + 1]
                    near = middle[k] + middle[k + 2]
                    near = near + state[held, x + k, start - 1 : start + size - 1, :]
                    near = near + state[held, x + k, start + 1 : start + size + 1, :]
                    new = q + dwide[x + k, start : start + size, :] * (near - 4.0 * q)
                    if last:
                        at = pl.multiple_of((x + k - 4) * WY, WY) + start - 16
                        profiles[pl.ds(pl.multiple_of(at, 8), size), :] = new
                    else:
                        state[following, x + k, start : start + size, :] = new
            return carry

        lax.fori_loop(0, count, rows, 0)

    def network(group, carry):
        rows = recv[pl.ds(group * GROUP, GROUP)].reshape(GROUP * CAP, FEATURES)
        center = jnp.mean(rows, axis=-1, keepdims=True)
        shifted = rows - center
        spread = jnp.mean(shifted * shifted, axis=-1, keepdims=True)
        rows = shifted * lax.rsqrt(spread + 1e-05)
        hidden = silu(product(rows, w1h, w1l))
        hidden = silu(product(hidden, w2h, w2l))
        hidden = silu(product(hidden, w3h, w3l))
        result = product(hidden, w4h, w4l)
        answer[pl.ds(group * GROUP, GROUP)] = result.reshape(GROUP, CAP, FEATURES)
        for part in range(TURNS):
            for lane in range(8):
                turn_number = group * TURNS + part
                step = turn_number * 8 + lane
                other = source(turn_number, lane)
                if part == 0 and lane == 0:

                    @pl.when(group > 0)
                    def _():
                        back(step, other).start()
                else:
                    back(step, other).start()
        return carry

    def arrived(first, count, group):
        pltpu.make_async_remote_copy(
            src_ref=recv.at[pl.ds(first, count)],
            dst_ref=recv.at[pl.ds(first, count)],
            send_sem=out_send,
            recv_sem=out_recv.at[group],
            device_id=me,
            device_id_type=LOGICAL,
        ).wait_recv()

    def arrived_network(group, carry):
        @pl.when(group == 0)
        def _():
            arrived(1, GROUP - 1, 0)

        @pl.when(group > 0)
        def _():
            arrived(group * GROUP, GROUP, group)

        network(group, carry)

        return carry

    lax.fori_loop(0, GROUPS, arrived_network, 0)
    own_answer = pltpu.make_async_copy(answer.at[0], drag_hbm.at[me], own_sem)
    own_answer.start()
    receive_halo()
    lax.fori_loop(0, ROWS_X // 4, widen, 0)
    diffuse(0)
    diffuse(1)
    diffuse(2)
    diffuse(3)
    diffused = pltpu.make_async_copy(profiles, diffused_hbm, diffused_sem)
    diffused.start()

    others = DEVICES - 1
    pltpu.make_async_remote_copy(
        src_ref=answer.at[pl.ds(0, others)],
        dst_ref=drag_hbm.at[pl.ds(0, others)],
        send_sem=back_send,
        recv_sem=back_recv,
        device_id=me,
        device_id_type=LOGICAL,
    ).wait()
    pltpu.make_async_remote_copy(
        src_ref=send.at[pl.ds(0, others)],
        dst_ref=recv.at[pl.ds(0, others)],
        send_sem=out_send,
        recv_sem=out_recv.at[0],
        device_id=me,
        device_id_type=LOGICAL,
    ).wait_send()
    diffused.wait()
    own_answer.wait()


def drag_and_diffusion(regimes, active_columns, u_field, v_field, diffusivity, layers):
    vmem = pl.BlockSpec(memory_space=pltpu.VMEM)
    hbm = pl.BlockSpec(memory_space=pltpu.HBM)
    shapes = [layer.shape[1:] for layer in layers]
    halves = [pltpu.VMEM(shape, BF16) for shape in shapes for _ in range(2)]
    dma = pltpu.SemaphoreType.DMA
    return pl.pallas_call(
        main_kernel,
        out_shape=(
            jax.ShapeDtypeStruct((DEVICES, CAP, FEATURES), F32),
            jax.ShapeDtypeStruct((WX * WY, FEATURES), F32),
            jax.ShapeDtypeStruct((1, ACTIVE), jnp.int32),
        ),
        in_specs=[vmem, vmem] + [hbm] * 7,
        out_specs=(hbm, hbm, vmem),
        scratch_shapes=[
            pltpu.VMEM((CAP, DEVICES), jnp.int32),
            pltpu.SMEM((CAP, DEVICES), jnp.int32),
            pltpu.VMEM((2, LEVELS, PADDED, WY), F32),
            pltpu.VMEM((WX * WY, FEATURES), F32),
            pltpu.VMEM((2, ROWS_X, ROWS_Y, FEATURES), F32),
            pltpu.VMEM((3, WX + 16, WY), F32),
            pltpu.VMEM((16, WY), F32),
            pltpu.VMEM((ROWS_X, ROWS_Y, FEATURES), F32),
            pltpu.VMEM((DEVICES, CAP, FEATURES), F32),
            pltpu.VMEM((DEVICES, CAP, FEATURES), F32),
            pltpu.VMEM((DEVICES, CAP, FEATURES), F32),
            *[pltpu.VMEM(shape, F32) for shape in shapes],
            *halves,
            dma((4, 2)),
            dma,
            dma((4,)),
            dma((8,)),
            dma((8,)),
            dma((8,)),
            dma((8,)),
            dma,
            dma((GROUPS,)),
            dma,
            dma,
            dma,
            dma,
        ],
        compiler_params=pltpu.CompilerParams(
            collective_id=0, has_side_effects=True, vmem_limit_bytes=59840 << 10
        ),
    )(regimes.reshape(1, ACTIVE), active_columns.reshape(1, ACTIVE), u_field, v_field, diffusivity, *layers)


def place_kernel(
    column_ref, slot_ref, drag_hbm, diffused_hbm, u_hbm, v_hbm, drag, dense, diffused, staged, drag_sem, in_sem, out_sem
):
    pieces = 4
    wide = WX // pieces
    drag_load = pltpu.make_async_copy(drag_hbm, drag, drag_sem)
    drag_load.start()
    loads = []
    for piece in range(pieces):
        part = pl.ds(piece * wide * WY, wide * WY)
        load = pltpu.make_async_copy(diffused_hbm.at[part], diffused.at[part], in_sem.at[piece])
        loads.append(load)

    def clear(x, carry):
        dense[pl.ds(pl.multiple_of(x * WY, WY), WY), :] = jnp.zeros((WY, FEATURES), F32)
        return carry

    lax.fori_loop(0, WX, clear, 0)
    drag_load.wait()
    for load in loads:
        load.start()
    drags = drag.reshape(DEVICES * CAP, FEATURES)

    def place(step, carry):
        rows = [drags[pl.ds(slot_ref[0, step * 32 + k], 1), :] for k in range(32)]
        for k in range(32):
            dense[pl.ds(column_ref[step * 32 + k], 1), :] = rows[k]
        return carry

    lax.fori_loop(0, ACTIVE // 32, place, 0)
    flat = staged.reshape(2 * LEVELS * PADDED, WY)

    def turn(step, carry):
        for k in range(8):
            x = 8 * step + k
            part = pl.ds(pl.multiple_of(x * WY, WY), WY)
            block = dense[part, :] + diffused[part, :]
            flat[pl.ds(x, FEATURES, stride=PADDED), :] = block.T
        return carry

    copies = []
    for piece in range(pieces):
        loads[piece].wait()
        lax.fori_loop(piece * wide // 8, (piece + 1) * wide // 8, turn, 0)
        part = pl.ds(piece * wide, wide)
        for which, target in enumerate((u_hbm, v_hbm)):
            copy = pltpu.make_async_copy(staged.at[which, :, part, :], target.at[:, part, :], out_sem.at[piece, which])
            copy.start()
            copies.append(copy)
    for copy in copies:
        copy.wait()


def place_drag(active_columns, slots, drag, diffused):
    smem = pl.BlockSpec(memory_space=pltpu.SMEM)
    hbm = pl.BlockSpec(memory_space=pltpu.HBM)
    shape = jax.ShapeDtypeStruct((LEVELS, WX, WY), F32)
    return pl.pallas_call(
        place_kernel,
        out_shape=(shape, shape),
        in_specs=[smem, smem, hbm, hbm],
        out_specs=(hbm, hbm),
        scratch_shapes=[
            pltpu.VMEM((DEVICES, CAP, FEATURES), F32),
            pltpu.VMEM((WX * WY, FEATURES), F32),
            pltpu.VMEM((WX * WY, FEATURES), F32),
            pltpu.VMEM((2, LEVELS, PADDED, WY), F32),
            pltpu.SemaphoreType.DMA,
            pltpu.SemaphoreType.DMA((4,)),
            pltpu.SemaphoreType.DMA((4, 2)),
        ],
        compiler_params=pltpu.CompilerParams(vmem_limit_bytes=59840 << 10),
    )(active_columns, slots, drag, diffused)


def body(
    u_field,
    v_field,
    diffusivity,
    active_columns,
    regimes,
    first_layer,
    second_layer,
    third_layer,
    last_layer,
):
    layers = (first_layer, second_layer, third_layer, last_layer)
    drag, diffused, slots = drag_and_diffusion(regimes, active_columns, u_field, v_field, diffusivity, layers)
    return place_drag(active_columns, slots, drag, diffused)


def solution(mesh):
    in_specs = (
        P(None, "tile", "inf"),
        P(None, "tile", "inf"),
        P("tile", "inf"),
        P(("tile", "inf")),
        P(("tile", "inf"), None),
        P(("tile", "inf"), None, None),
        P(("tile", "inf"), None, None),
        P(("tile", "inf"), None, None),
        P(("tile", "inf"), None, None),
    )
    out_specs = (P(None, "tile", "inf"), P(None, "tile", "inf"))
    return jax.shard_map(body, mesh=mesh, in_specs=in_specs, out_specs=out_specs, check_vma=False)
```

```python
import functools

import jax
import jax.numpy as jnp
from jax import lax
from jax.experimental import pallas as pl
from jax.experimental.pallas import tpu as pltpu
from jax.sharding import PartitionSpec as P

PASSES = 4
LOGICAL = pl.DeviceIdType.LOGICAL
F32 = jnp.float32
BF16 = jnp.bfloat16

LEVELS = 64
FEATURES = 128
WX = 64
WY = 128
CAP = 32
DEVICES = 128
ACTIVE = 2048
ROWS_X = WX + 8
ROWS_Y = WY + 32
GROUP = 32
PADDED = WX + 8
GROUPS = DEVICES // GROUP
TURNS = GROUP // 8
AHEAD = 3


def find_slots(regime_ref, column_ref, pick_ref, slot_ref):
    width = 256
    blocks = ACTIVE // width
    expert = lax.broadcasted_iota(jnp.int32, (DEVICES, width), 0)
    earlier = lax.broadcasted_iota(jnp.int32, (width, width), 0)
    later = lax.broadcasted_iota(jnp.int32, (width, width), 1)
    upper = (earlier < later).astype(BF16)
    place = lax.broadcasted_iota(jnp.int32, (CAP, width), 0)
    counts = jnp.zeros((DEVICES, 1), F32)
    pick_x = jnp.zeros((CAP, DEVICES), F32)
    pick_y = jnp.zeros((CAP, DEVICES), F32)
    for block in range(blocks):
        part = slice(block * width, (block + 1) * width)
        named = regime_ref[:, part]
        column = column_ref[:, part]
        hit = (expert == named).astype(F32)
        hit16 = hit.astype(BF16)
        before = jnp.dot(hit16, upper, preferred_element_type=F32) + counts
        rank = jnp.sum(before * hit, axis=0, keepdims=True).astype(jnp.int32)
        counts = counts + jnp.sum(hit, axis=1, keepdims=True)
        slot_ref[:, part] = named * CAP + rank
        chosen = (place == rank).astype(F32)
        x = (column // WY).astype(F32)
        y = (column % WY).astype(F32)
        dims = (((1,), (1,)), ((), ()))
        pick_x = pick_x + lax.dot_general((chosen * x).astype(BF16), hit16, dims, preferred_element_type=F32)
        pick_y = pick_y + lax.dot_general((chosen * y).astype(BF16), hit16, dims, preferred_element_type=F32)
    pick_ref[...] = jnp.clip((pick_x * WY + pick_y).astype(jnp.int32), 0, WX * WY - 1)


NEIGHBOURS = [(dx, dy) for dx in (-1, 0, 1) for dy in (-1, 0, 1) if (dx, dy) != (0, 0)]


def split(value):
    high = value.astype(BF16)
    return high, (value - high.astype(F32)).astype(BF16)


def product(rows, high_ref, low_ref):
    high, low = split(rows)
    total = jnp.dot(high, low_ref[...], preferred_element_type=F32)
    total = total + jnp.dot(low, high_ref[...], preferred_element_type=F32)
    return total + jnp.dot(high, high_ref[...], preferred_element_type=F32)


def silu(z):
    half = 0.5 * z
    return half + half * jnp.tanh(half)


def main_kernel(
    regime_ref,
    column_ref,
    u_hbm,
    v_hbm,
    d_hbm,
    w1_hbm,
    w2_hbm,
    w3_hbm,
    w4_hbm,
    drag_hbm,
    diffused_hbm,
    slot_ref,
    pick_vmem,
    pick_ref,
    fields,
    profiles,
    state,
    dext,
    sides_ref,
    dwide,
    send,
    recv,
    answer,
    w1,
    w2,
    w3,
    w4,
    w1h,
    w1l,
    w2h,
    w2l,
    w3h,
    w3l,
    w4h,
    w4l,
    load_sem,
    own_sem,
    weight_sem,
    halo_send,
    halo_recv,
    dhalo_send,
    dhalo_recv,
    out_send,
    out_recv,
    back_send,
    back_recv,
    diffused_sem,
    pick_sem,
):
    tile = lax.axis_index("tile")
    inf = lax.axis_index("inf")
    me = tile * 8 + inf
    at_x, at_z = tile // 4, tile % 4
    at_y, at_c = inf // 2, inf % 2

    pieces = 4
    wide = WX // pieces
    loads = []
    for piece in range(pieces):
        part = pl.ds(piece * wide, wide)
        for which, source in enumerate((u_hbm, v_hbm)):
            loads.append(
                pltpu.make_async_copy(source.at[:, part, :], fields.at[which, :, part, :], load_sem.at[piece, which])
            )
    own_d = pltpu.make_async_copy(d_hbm, dext.at[1, pl.ds(8, WX), :], own_sem)
    weight_loads = [
        pltpu.make_async_copy(source.at[0], target, weight_sem.at[number])
        for number, (source, target) in enumerate(((w1_hbm, w1), (w2_hbm, w2), (w3_hbm, w3), (w4_hbm, w4)))
    ]
    for load in loads:
        load.start()
    own_d.start()
    for load in weight_loads:
        load.start()

    barrier = pltpu.get_barrier_semaphore()

    def greet(step, carry):
        other = me + step
        other = jnp.where(other >= DEVICES, other - DEVICES, other)
        pl.semaphore_signal(barrier, inc=1, device_id=other, device_id_type=LOGICAL)
        return carry

    lax.fori_loop(1, DEVICES, greet, 0)

    find_slots(regime_ref, column_ref, pick_vmem, slot_ref)
    picks = pltpu.make_async_copy(pick_vmem, pick_ref, pick_sem)
    picks.start()

    flat_fields = fields.reshape(2 * LEVELS * PADDED, WY)

    def turn(step, carry):
        for k in range(4):
            x = 4 * step + k
            block = flat_fields[pl.ds(x, FEATURES, stride=PADDED), :].T
            state[0, x + 4, 16 : 16 + WY, :] = block
            profiles[pl.ds(pl.multiple_of(x * WY, WY), WY), :] = block
        return carry

    for piece in range(pieces):
        loads[2 * piece].wait()
        loads[2 * piece + 1].wait()
        lax.fori_loop(piece * wide // 4, (piece + 1) * wide // 4, turn, 0)
    own_d.wait()
    picks.wait()

    @pl.when(tile == 0)
    def _():
        state[0, 0:4, 8 : 24 + WY, :] = jnp.zeros((4, WY + 16, FEATURES), F32)
        dext[:, 0:8, :] = jnp.zeros((3, 8, WY), F32)

    @pl.when(tile == 15)
    def _():
        state[0, WX + 4 : WX + 8, 8 : 24 + WY, :] = jnp.zeros((4, WY + 16, FEATURES), F32)
        dext[:, WX + 8 : WX + 16, :] = jnp.zeros((3, 8, WY), F32)

    @pl.when(inf == 0)
    def _():
        state[0, :, 8:16, :] = jnp.zeros((ROWS_X, 8, FEATURES), F32)
        dext[0, :, :] = jnp.zeros((WX + 16, WY), F32)

    @pl.when(inf == 7)
    def _():
        state[0, :, 16 + WY : 24 + WY, :] = jnp.zeros((ROWS_X, 8, FEATURES), F32)
        dext[2, :, :] = jnp.zeros((WX + 16, WY), F32)

    pl.semaphore_wait(barrier, DEVICES - 1)

    def halo(number):
        dx, dy = NEIGHBOURS[number]
        opposite = NEIGHBOURS.index((-dx, -dy))
        there_x, there_y = tile + dx, inf + dy
        exists = (there_x >= 0) & (there_x < 16) & (there_y >= 0) & (there_y < 8)
        comes_x, comes_y = tile - dx, inf - dy
        comes = (comes_x >= 0) & (comes_x < 16) & (comes_y >= 0) & (comes_y < 8)
        from_x = {1: pl.ds(WX, 4), -1: pl.ds(4, 4), 0: pl.ds(4, WX)}[dx]
        to_x = {1: pl.ds(0, 4), -1: pl.ds(WX + 4, 4), 0: pl.ds(4, WX)}[dx]
        from_y = {1: pl.ds(8 + WY, 8), -1: pl.ds(16, 8), 0: pl.ds(16, WY)}[dy]
        to_y = {1: pl.ds(8, 8), -1: pl.ds(16 + WY, 8), 0: pl.ds(16, WY)}[dy]
        from_d = {1: pl.ds(WX, 8), -1: pl.ds(8, 8), 0: pl.ds(8, WX)}[dx]
        to_d = {1: pl.ds(0, 8), -1: pl.ds(WX + 8, 8), 0: pl.ds(8, WX)}[dx]
        other = there_x * 8 + there_y
        profile = pltpu.make_async_remote_copy(
            src_ref=state.at[0, from_x, from_y, :],
            dst_ref=state.at[0, to_x, to_y, :],
            send_sem=halo_send.at[number],
            recv_sem=halo_recv.at[number],
            device_id=other,
            device_id_type=LOGICAL,
        )
        number_d = pltpu.make_async_remote_copy(
            src_ref=dext.at[1, from_d, :],
            dst_ref=dext.at[1 - dy, to_d, :],
            send_sem=dhalo_send.at[number],
            recv_sem=dhalo_recv.at[number],
            device_id=other,
            device_id_type=LOGICAL,
        )
        return exists, comes, profile, number_d

    for number in range(8):
        exists, _, profile, coefficient = halo(number)

        @pl.when(exists)
        def _():
            coefficient.start()
            profile.start()

    def target(turn_number, lane):
        x = (at_x + lane) % 4
        c = (at_c + lane // 4) % 2
        z = (at_z + lane + turn_number) % 4
        y = (at_y + lane + turn_number // 4) % 4
        return x * 32 + z * 8 + y * 2 + c

    def source(turn_number, lane):
        x = (at_x + 8 - lane) % 4
        c = (at_c + 2 - lane // 4) % 2
        z = (at_z + 24 - lane - turn_number) % 4
        y = (at_y + 12 - lane - turn_number // 4) % 4
        return x * 32 + z * 8 + y * 2 + c

    def away(step, other, group):
        return pltpu.make_async_remote_copy(
            src_ref=send.at[step],
            dst_ref=recv.at[step],
            send_sem=out_send,
            recv_sem=out_recv.at[group],
            device_id=other,
            device_id_type=LOGICAL,
        )

    def back(step, other):
        return pltpu.make_async_remote_copy(
            src_ref=answer.at[step],
            dst_ref=drag_hbm.at[me],
            send_sem=back_send,
            recv_sem=back_recv,
            device_id=other,
            device_id_type=LOGICAL,
        )

    def dispatch(turn_number, carry):
        for lane in range(8):
            step = turn_number * 8 + lane
            other = target(turn_number, lane)
            for k in range(CAP):
                row = pick_ref[k, other]
                send[step, k : k + 1, :] = profiles[pl.ds(row, 1), :]
            if lane == 0:

                @pl.when(turn_number > 0)
                def _():
                    away(step, other, turn_number // TURNS).start()
            else:
                away(step, other, turn_number // TURNS).start()
        return carry

    lax.fori_loop(0, AHEAD * TURNS, dispatch, 0)
    recv[0] = send[0]

    for load in weight_loads:
        load.wait()
    for whole, high_ref, low_ref in ((w1, w1h, w1l), (w2, w2h, w2l), (w3, w3h, w3l), (w4, w4h, w4l)):
        high, low = split(whole[...])
        high_ref[...] = high
        low_ref[...] = low

    def receive_halo():
        for number in range(8):
            exists, comes, profile, coefficient = halo(number)

            @pl.when(comes)
            def _():
                coefficient.wait_recv()
                profile.wait_recv()

            @pl.when(exists)
            def _():
                coefficient.wait_send()
                profile.wait_send()

        lane = lax.broadcasted_iota(jnp.int32, (WX + 16, WY), 1)
        left = pltpu.roll(dext[0], 8, 1)
        right = pltpu.roll(dext[2], 8, 1)
        sides = jnp.where(lane < 8, left, right)
        sides_ref[...] = jnp.concatenate([sides, jnp.zeros((WY - WX - 16, WY), F32)], axis=0).T[0:16, :]

    def widen(step, carry):
        for k in range(4):
            x = 4 * step + k
            row = dext[1, pl.ds(x + 4, 1), :]
            dwide[x, 16 : 16 + WY, :] = jnp.broadcast_to(row, (WY, FEATURES)).T
            column = pltpu.roll(sides_ref[...], WY - 4 - x, 1)[:, 0:1]
            column = jnp.broadcast_to(column, (16, FEATURES))
            dwide[x, 8:16, :] = column[0:8]
            dwide[x, 16 + WY : 24 + WY, :] = column[8:16]
        return carry

    def diffuse(number):
        held, following = number % 2, 1 - number % 2
        last = number == PASSES - 1
        first = number + 1
        count = (ROWS_X - 2 * first) // 2
        cuts = [(16 + 64 * cut, 64) for cut in range(2)] if last else [(8 + 48 * cut, 48) for cut in range(3)]

        def rows(step, carry):
            x = first + 2 * step
            for start, size in cuts:
                middle = [state[held, x - 1 + k, start : start + size, :] for k in range(4)]
                for k in range(2):
                    q = middle[k + 1]
                    near = middle[k] + middle[k + 2]
                    near = near + state[held, x + k, start - 1 : start + size - 1, :]
                    near = near + state[held, x + k, start + 1 : start + size + 1, :]
                    new = q + dwide[x + k, start : start + size, :] * (near - 4.0 * q)
                    if last:
                        at = pl.multiple_of((x + k - 4) * WY, WY) + start - 16
                        profiles[pl.ds(pl.multiple_of(at, 8), size), :] = new
                    else:
                        state[following, x + k, start : start + size, :] = new
            return carry

        lax.fori_loop(0, count, rows, 0)

    def network(group, carry):
        rows = recv[pl.ds(group * GROUP, GROUP)].reshape(GROUP * CAP, FEATURES)
        center = jnp.mean(rows, axis=-1, keepdims=True)
        shifted = rows - center
        spread = jnp.mean(shifted * shifted, axis=-1, keepdims=True)
        rows = shifted * lax.rsqrt(spread + 1e-05)
        hidden = silu(product(rows, w1h, w1l))
        hidden = silu(product(hidden, w2h, w2l))
        hidden = silu(product(hidden, w3h, w3l))
        result = product(hidden, w4h, w4l)
        answer[pl.ds(group * GROUP, GROUP)] = result.reshape(GROUP, CAP, FEATURES)
        for part in range(TURNS):
            for lane in range(8):
                turn_number = group * TURNS + part
                step = turn_number * 8 + lane
                other = source(turn_number, lane)
                if part == 0 and lane == 0:

                    @pl.when(group > 0)
                    def _():
                        back(step, other).start()
                else:
                    back(step, other).start()
        return carry

    def arrived(first, count, group):
        pltpu.make_async_remote_copy(
            src_ref=recv.at[pl.ds(first, count)],
            dst_ref=recv.at[pl.ds(first, count)],
            send_sem=out_send,
            recv_sem=out_recv.at[group],
            device_id=me,
            device_id_type=LOGICAL,
        ).wait_recv()

    def arrived_network(group, carry):
        @pl.when(group == 0)
        def _():
            arrived(1, GROUP - 1, 0)

        @pl.when(group > 0)
        def _():
            arrived(group * GROUP, GROUP, group)

        @pl.when(group < GROUPS - AHEAD)
        def _():
            first = (group + AHEAD) * TURNS
            lax.fori_loop(first, first + TURNS, dispatch, 0)

        network(group, carry)

        return carry

    lax.fori_loop(0, GROUPS, arrived_network, 0)
    own_answer = pltpu.make_async_copy(answer.at[0], drag_hbm.at[me], own_sem)
    own_answer.start()
    receive_halo()
    lax.fori_loop(0, ROWS_X // 4, widen, 0)
    diffuse(0)
    diffuse(1)
    diffuse(2)
    diffuse(3)
    diffused = pltpu.make_async_copy(profiles, diffused_hbm, diffused_sem)
    diffused.start()

    others = DEVICES - 1
    pltpu.make_async_remote_copy(
        src_ref=answer.at[pl.ds(0, others)],
        dst_ref=drag_hbm.at[pl.ds(0, others)],
        send_sem=back_send,
        recv_sem=back_recv,
        device_id=me,
        device_id_type=LOGICAL,
    ).wait()
    pltpu.make_async_remote_copy(
        src_ref=send.at[pl.ds(0, others)],
        dst_ref=recv.at[pl.ds(0, others)],
        send_sem=out_send,
        recv_sem=out_recv.at[0],
        device_id=me,
        device_id_type=LOGICAL,
    ).wait_send()
    diffused.wait()
    own_answer.wait()


def drag_and_diffusion(regimes, active_columns, u_field, v_field, diffusivity, layers):
    vmem = pl.BlockSpec(memory_space=pltpu.VMEM)
    hbm = pl.BlockSpec(memory_space=pltpu.HBM)
    shapes = [layer.shape[1:] for layer in layers]
    halves = [pltpu.VMEM(shape, BF16) for shape in shapes for _ in range(2)]
    dma = pltpu.SemaphoreType.DMA
    return pl.pallas_call(
        main_kernel,
        out_shape=(
            jax.ShapeDtypeStruct((DEVICES, CAP, FEATURES), F32),
            jax.ShapeDtypeStruct((WX * WY, FEATURES), F32),
            jax.ShapeDtypeStruct((1, ACTIVE), jnp.int32),
        ),
        in_specs=[vmem, vmem] + [hbm] * 7,
        out_specs=(hbm, hbm, vmem),
        scratch_shapes=[
            pltpu.VMEM((CAP, DEVICES), jnp.int32),
            pltpu.SMEM((CAP, DEVICES), jnp.int32),
            pltpu.VMEM((2, LEVELS, PADDED, WY), F32),
            pltpu.VMEM((WX * WY, FEATURES), F32),
            pltpu.VMEM((2, ROWS_X, ROWS_Y, FEATURES), F32),
            pltpu.VMEM((3, WX + 16, WY), F32),
            pltpu.VMEM((16, WY), F32),
            pltpu.VMEM((ROWS_X, ROWS_Y, FEATURES), F32),
            pltpu.VMEM((DEVICES, CAP, FEATURES), F32),
            pltpu.VMEM((DEVICES, CAP, FEATURES), F32),
            pltpu.VMEM((DEVICES, CAP, FEATURES), F32),
            *[pltpu.VMEM(shape, F32) for shape in shapes],
            *halves,
            dma((4, 2)),
            dma,
            dma((4,)),
            dma((8,)),
            dma((8,)),
            dma((8,)),
            dma((8,)),
            dma,
            dma((GROUPS,)),
            dma,
            dma,
            dma,
            dma,
        ],
        compiler_params=pltpu.CompilerParams(
            collective_id=0, has_side_effects=True, vmem_limit_bytes=59840 << 10
        ),
    )(regimes.reshape(1, ACTIVE), active_columns.reshape(1, ACTIVE), u_field, v_field, diffusivity, *layers)


def place_kernel(
    column_ref, slot_ref, drag_hbm, diffused_hbm, u_hbm, v_hbm, drag, dense, diffused, staged, drag_sem, in_sem, out_sem
):
    pieces = 4
    wide = WX // pieces
    drag_load = pltpu.make_async_copy(drag_hbm, drag, drag_sem)
    drag_load.start()
    loads = []
    for piece in range(pieces):
        part = pl.ds(piece * wide * WY, wide * WY)
        load = pltpu.make_async_copy(diffused_hbm.at[part], diffused.at[part], in_sem.at[piece])
        loads.append(load)

    def clear(x, carry):
        dense[pl.ds(pl.multiple_of(x * WY, WY), WY), :] = jnp.zeros((WY, FEATURES), F32)
        return carry

    lax.fori_loop(0, WX, clear, 0)
    drag_load.wait()
    for load in loads:
        load.start()
    drags = drag.reshape(DEVICES * CAP, FEATURES)

    def place(step, carry):
        rows = [drags[pl.ds(slot_ref[0, step * 32 + k], 1), :] for k in range(32)]
        for k in range(32):
            dense[pl.ds(column_ref[step * 32 + k], 1), :] = rows[k]
        return carry

    lax.fori_loop(0, ACTIVE // 32, place, 0)
    flat = staged.reshape(2 * LEVELS * PADDED, WY)

    def turn(step, carry):
        for k in range(8):
            x = 8 * step + k
            part = pl.ds(pl.multiple_of(x * WY, WY), WY)
            block = dense[part, :] + diffused[part, :]
            flat[pl.ds(x, FEATURES, stride=PADDED), :] = block.T
        return carry

    copies = []
    for piece in range(pieces):
        loads[piece].wait()
        lax.fori_loop(piece * wide // 8, (piece + 1) * wide // 8, turn, 0)
        part = pl.ds(piece * wide, wide)
        for which, target in enumerate((u_hbm, v_hbm)):
            copy = pltpu.make_async_copy(staged.at[which, :, part, :], target.at[:, part, :], out_sem.at[piece, which])
            copy.start()
            copies.append(copy)
    for copy in copies:
        copy.wait()


def place_drag(active_columns, slots, drag, diffused):
    smem = pl.BlockSpec(memory_space=pltpu.SMEM)
    hbm = pl.BlockSpec(memory_space=pltpu.HBM)
    shape = jax.ShapeDtypeStruct((LEVELS, WX, WY), F32)
    return pl.pallas_call(
        place_kernel,
        out_shape=(shape, shape),
        in_specs=[smem, smem, hbm, hbm],
        out_specs=(hbm, hbm),
        scratch_shapes=[
            pltpu.VMEM((DEVICES, CAP, FEATURES), F32),
            pltpu.VMEM((WX * WY, FEATURES), F32),
            pltpu.VMEM((WX * WY, FEATURES), F32),
            pltpu.VMEM((2, LEVELS, PADDED, WY), F32),
            pltpu.SemaphoreType.DMA,
            pltpu.SemaphoreType.DMA((4,)),
            pltpu.SemaphoreType.DMA((4, 2)),
        ],
        compiler_params=pltpu.CompilerParams(vmem_limit_bytes=59840 << 10),
    )(active_columns, slots, drag, diffused)


def body(
    u_field,
    v_field,
    diffusivity,
    active_columns,
    regimes,
    first_layer,
    second_layer,
    third_layer,
    last_layer,
):
    layers = (first_layer, second_layer, third_layer, last_layer)
    drag, diffused, slots = drag_and_diffusion(regimes, active_columns, u_field, v_field, diffusivity, layers)
    return place_drag(active_columns, slots, drag, diffused)


def solution(mesh):
    in_specs = (
        P(None, "tile", "inf"),
        P(None, "tile", "inf"),
        P("tile", "inf"),
        P(("tile", "inf")),
        P(("tile", "inf"), None),
        P(("tile", "inf"), None, None),
        P(("tile", "inf"), None, None),
        P(("tile", "inf"), None, None),
        P(("tile", "inf"), None, None),
    )
    out_specs = (P(None, "tile", "inf"), P(None, "tile", "inf"))
    return jax.shard_map(body, mesh=mesh, in_specs=in_specs, out_specs=out_specs, check_vma=False)
```

```python
import functools

import jax
import jax.numpy as jnp
from jax import lax
from jax.experimental import pallas as pl
from jax.experimental.pallas import tpu as pltpu
from jax.sharding import PartitionSpec as P

PASSES = 4
LOGICAL = pl.DeviceIdType.LOGICAL
F32 = jnp.float32
BF16 = jnp.bfloat16

LEVELS = 64
FEATURES = 128
WX = 64
WY = 128
CAP = 32
DEVICES = 128
ACTIVE = 2048
ROWS_X = WX + 8
ROWS_Y = WY + 32
GROUP = 32
PADDED = WX + 8
GROUPS = DEVICES // GROUP
TURNS = GROUP // 8
AHEAD = 3


def find_slots(regime_ref, column_ref, pick_ref, slot_ref):
    width = 256
    blocks = ACTIVE // width
    expert = lax.broadcasted_iota(jnp.int32, (DEVICES, width), 0)
    earlier = lax.broadcasted_iota(jnp.int32, (width, width), 0)
    later = lax.broadcasted_iota(jnp.int32, (width, width), 1)
    upper = (earlier < later).astype(BF16)
    place = lax.broadcasted_iota(jnp.int32, (CAP, width), 0)
    counts = jnp.zeros((DEVICES, 1), F32)
    pick_x = jnp.zeros((CAP, DEVICES), F32)
    pick_y = jnp.zeros((CAP, DEVICES), F32)
    for block in range(blocks):
        part = slice(block * width, (block + 1) * width)
        named = regime_ref[:, part]
        column = column_ref[:, part]
        hit = (expert == named).astype(F32)
        hit16 = hit.astype(BF16)
        before = jnp.dot(hit16, upper, preferred_element_type=F32) + counts
        rank = jnp.sum(before * hit, axis=0, keepdims=True).astype(jnp.int32)
        counts = counts + jnp.sum(hit, axis=1, keepdims=True)
        slot_ref[:, part] = named * CAP + rank
        chosen = (place == rank).astype(F32)
        x = (column // WY).astype(F32)
        y = (column % WY).astype(F32)
        dims = (((1,), (1,)), ((), ()))
        pick_x = pick_x + lax.dot_general((chosen * x).astype(BF16), hit16, dims, preferred_element_type=F32)
        pick_y = pick_y + lax.dot_general((chosen * y).astype(BF16), hit16, dims, preferred_element_type=F32)
    pick_ref[...] = jnp.clip((pick_x * WY + pick_y).astype(jnp.int32), 0, WX * WY - 1)


NEIGHBOURS = [(dx, dy) for dx in (-1, 0, 1) for dy in (-1, 0, 1) if (dx, dy) != (0, 0)]


def split(value):
    high = value.astype(BF16)
    return high, (value - high.astype(F32)).astype(BF16)


def product(rows, high_ref, low_ref):
    high, low = split(rows)
    total = jnp.dot(high, low_ref[...], preferred_element_type=F32)
    total = total + jnp.dot(low, high_ref[...], preferred_element_type=F32)
    return total + jnp.dot(high, high_ref[...], preferred_element_type=F32)


def silu(z):
    half = 0.5 * z
    return half + half * jnp.tanh(half)


def main_kernel(
    regime_ref,
    column_ref,
    u_hbm,
    v_hbm,
    d_hbm,
    w1_hbm,
    w2_hbm,
    w3_hbm,
    w4_hbm,
    drag_hbm,
    diffused_hbm,
    slot_ref,
    pick_vmem,
    pick_ref,
    fields,
    profiles,
    state,
    dext,
    sides_ref,
    dwide,
    send,
    recv,
    answer,
    w1,
    w2,
    w3,
    w4,
    w1h,
    w1l,
    w2h,
    w2l,
    w3h,
    w3l,
    w4h,
    w4l,
    load_sem,
    own_sem,
    weight_sem,
    halo_send,
    halo_recv,
    dhalo_send,
    dhalo_recv,
    out_send,
    out_recv,
    back_send,
    back_recv,
    diffused_sem,
    pick_sem,
):
    tile = lax.axis_index("tile")
    inf = lax.axis_index("inf")
    me = tile * 8 + inf
    at_x, at_z = tile // 4, tile % 4
    at_y, at_c = inf // 2, inf % 2

    pieces = 4
    wide = WX // pieces
    loads = []
    for piece in range(pieces):
        part = pl.ds(piece * wide, wide)
        for which, source in enumerate((u_hbm, v_hbm)):
            loads.append(
                pltpu.make_async_copy(source.at[:, part, :], fields.at[which, :, part, :], load_sem.at[piece, which])
            )
    own_d = pltpu.make_async_copy(d_hbm, dext.at[1, pl.ds(8, WX), :], own_sem)
    weight_loads = [
        pltpu.make_async_copy(source.at[0], target, weight_sem.at[number])
        for number, (source, target) in enumerate(((w1_hbm, w1), (w2_hbm, w2), (w3_hbm, w3), (w4_hbm, w4)))
    ]
    for load in loads:
        load.start()
    own_d.start()
    for load in weight_loads:
        load.start()

    barrier = pltpu.get_barrier_semaphore()

    def greet(step, carry):
        other = me + step
        other = jnp.where(other >= DEVICES, other - DEVICES, other)
        pl.semaphore_signal(barrier, inc=1, device_id=other, device_id_type=LOGICAL)
        return carry

    lax.fori_loop(1, DEVICES, greet, 0)

    find_slots(regime_ref, column_ref, pick_vmem, slot_ref)
    picks = pltpu.make_async_copy(pick_vmem, pick_ref, pick_sem)
    picks.start()

    flat_fields = fields.reshape(2 * LEVELS * PADDED, WY)

    def turn(step, carry):
        for k in range(4):
            x = 4 * step + k
            block = flat_fields[pl.ds(x, FEATURES, stride=PADDED), :].T
            state[0, x + 4, 16 : 16 + WY, :] = block
            profiles[pl.ds(pl.multiple_of(x * WY, WY), WY), :] = block
        return carry

    for piece in range(pieces):
        loads[2 * piece].wait()
        loads[2 * piece + 1].wait()
        lax.fori_loop(piece * wide // 4, (piece + 1) * wide // 4, turn, 0)
    own_d.wait()
    picks.wait()

    @pl.when(tile == 0)
    def _():
        state[0, 0:4, 8 : 24 + WY, :] = jnp.zeros((4, WY + 16, FEATURES), F32)
        dext[:, 0:8, :] = jnp.zeros((3, 8, WY), F32)

    @pl.when(tile == 15)
    def _():
        state[0, WX + 4 : WX + 8, 8 : 24 + WY, :] = jnp.zeros((4, WY + 16, FEATURES), F32)
        dext[:, WX + 8 : WX + 16, :] = jnp.zeros((3, 8, WY), F32)

    @pl.when(inf == 0)
    def _():
        state[0, :, 8:16, :] = jnp.zeros((ROWS_X, 8, FEATURES), F32)
        dext[0, :, :] = jnp.zeros((WX + 16, WY), F32)

    @pl.when(inf == 7)
    def _():
        state[0, :, 16 + WY : 24 + WY, :] = jnp.zeros((ROWS_X, 8, FEATURES), F32)
        dext[2, :, :] = jnp.zeros((WX + 16, WY), F32)

    pl.semaphore_wait(barrier, DEVICES - 1)

    def halo(number):
        dx, dy = NEIGHBOURS[number]
        opposite = NEIGHBOURS.index((-dx, -dy))
        there_x, there_y = tile + dx, inf + dy
        exists = (there_x >= 0) & (there_x < 16) & (there_y >= 0) & (there_y < 8)
        comes_x, comes_y = tile - dx, inf - dy
        comes = (comes_x >= 0) & (comes_x < 16) & (comes_y >= 0) & (comes_y < 8)
        from_x = {1: pl.ds(WX, 4), -1: pl.ds(4, 4), 0: pl.ds(4, WX)}[dx]
        to_x = {1: pl.ds(0, 4), -1: pl.ds(WX + 4, 4), 0: pl.ds(4, WX)}[dx]
        from_y = {1: pl.ds(8 + WY, 8), -1: pl.ds(16, 8), 0: pl.ds(16, WY)}[dy]
        to_y = {1: pl.ds(8, 8), -1: pl.ds(16 + WY, 8), 0: pl.ds(16, WY)}[dy]
        from_d = {1: pl.ds(WX, 8), -1: pl.ds(8, 8), 0: pl.ds(8, WX)}[dx]
        to_d = {1: pl.ds(0, 8), -1: pl.ds(WX + 8, 8), 0: pl.ds(8, WX)}[dx]
        other = there_x * 8 + there_y
        profile = pltpu.make_async_remote_copy(
            src_ref=state.at[0, from_x, from_y, :],
            dst_ref=state.at[0, to_x, to_y, :],
            send_sem=halo_send.at[number],
            recv_sem=halo_recv.at[number],
            device_id=other,
            device_id_type=LOGICAL,
        )
        number_d = pltpu.make_async_remote_copy(
            src_ref=dext.at[1, from_d, :],
            dst_ref=dext.at[1 - dy, to_d, :],
            send_sem=dhalo_send.at[number],
            recv_sem=dhalo_recv.at[number],
            device_id=other,
            device_id_type=LOGICAL,
        )
        return exists, comes, profile, number_d

    for number in range(8):
        exists, _, profile, coefficient = halo(number)

        @pl.when(exists)
        def _():
            coefficient.start()
            profile.start()

    def target(turn_number, lane):
        x = (at_x + lane) % 4
        c = (at_c + lane // 4) % 2
        z = (at_z + lane + turn_number) % 4
        y = (at_y + lane + turn_number // 4) % 4
        return x * 32 + z * 8 + y * 2 + c

    def source(turn_number, lane):
        x = (at_x + 8 - lane) % 4
        c = (at_c + 2 - lane // 4) % 2
        z = (at_z + 24 - lane - turn_number) % 4
        y = (at_y + 12 - lane - turn_number // 4) % 4
        return x * 32 + z * 8 + y * 2 + c

    def away(step, other, group):
        return pltpu.make_async_remote_copy(
            src_ref=send.at[step],
            dst_ref=recv.at[step],
            send_sem=out_send,
            recv_sem=out_recv.at[group],
            device_id=other,
            device_id_type=LOGICAL,
        )

    def back(step, other):
        return pltpu.make_async_remote_copy(
            src_ref=answer.at[step],
            dst_ref=drag_hbm.at[me],
            send_sem=back_send,
            recv_sem=back_recv,
            device_id=other,
            device_id_type=LOGICAL,
        )

    def dispatch(turn_number, carry):
        for lane in range(8):
            step = turn_number * 8 + lane
            other = target(turn_number, lane)
            for k in range(CAP):
                row = pick_ref[k, other]
                send[step, k : k + 1, :] = profiles[pl.ds(row, 1), :]
            if lane == 0:

                @pl.when(turn_number > 0)
                def _():
                    away(step, other, turn_number // TURNS).start()
            else:
                away(step, other, turn_number // TURNS).start()
        return carry

    lax.fori_loop(0, AHEAD * TURNS, dispatch, 0)
    recv[0] = send[0]

    for load in weight_loads:
        load.wait()
    for whole, high_ref, low_ref in ((w1, w1h, w1l), (w2, w2h, w2l), (w3, w3h, w3l), (w4, w4h, w4l)):
        high, low = split(whole[...])
        high_ref[...] = high
        low_ref[...] = low

    def receive_halo():
        for number in range(8):
            exists, comes, profile, coefficient = halo(number)

            @pl.when(comes)
            def _():
                coefficient.wait_recv()
                profile.wait_recv()

            @pl.when(exists)
            def _():
                coefficient.wait_send()
                profile.wait_send()

        lane = lax.broadcasted_iota(jnp.int32, (WX + 16, WY), 1)
        left = pltpu.roll(dext[0], 8, 1)
        right = pltpu.roll(dext[2], 8, 1)
        sides = jnp.where(lane < 8, left, right)
        sides_ref[...] = jnp.concatenate([sides, jnp.zeros((WY - WX - 16, WY), F32)], axis=0).T[0:16, :]

    def widen(step, carry):
        for k in range(4):
            x = 4 * step + k
            row = dext[1, pl.ds(x + 4, 1), :]
            dwide[x, 16 : 16 + WY, :] = jnp.broadcast_to(row, (WY, FEATURES)).T
            column = pltpu.roll(sides_ref[...], WY - 4 - x, 1)[:, 0:1]
            column = jnp.broadcast_to(column, (16, FEATURES))
            dwide[x, 8:16, :] = column[0:8]
            dwide[x, 16 + WY : 24 + WY, :] = column[8:16]
        return carry

    def diffuse(number):
        held, following = number % 2, 1 - number % 2
        last = number == PASSES - 1
        first = number + 1
        count = (ROWS_X - 2 * first) // 2
        cuts = [(16 + 64 * cut, 64) for cut in range(2)] if last else [(8 + 48 * cut, 48) for cut in range(3)]

        def rows(step, carry):
            x = first + 2 * step
            for start, size in cuts:
                middle = [state[held, x - 1 + k, start : start + size, :] for k in range(4)]
                for k in range(2):
                    q = middle[k + 1]
                    near = middle[k] + middle[k + 2]
                    near = near + state[held, x + k, start - 1 : start + size - 1, :]
                    near = near + state[held, x + k, start + 1 : start + size + 1, :]
                    new = q + dwide[x + k, start : start + size, :] * (near - 4.0 * q)
                    if last:
                        at = pl.multiple_of((x + k - 4) * WY, WY) + start - 16
                        profiles[pl.ds(pl.multiple_of(at, 8), size), :] = new
                    else:
                        state[following, x + k, start : start + size, :] = new
            return carry

        lax.fori_loop(0, count, rows, 0)

    def network(group, carry):
        rows = recv[pl.ds(group * GROUP, GROUP)].reshape(GROUP * CAP, FEATURES)
        center = jnp.mean(rows, axis=-1, keepdims=True)
        shifted = rows - center
        spread = jnp.mean(shifted * shifted, axis=-1, keepdims=True)
        rows = shifted * lax.rsqrt(spread + 1e-05)
        hidden = silu(product(rows, w1h, w1l))
        hidden = silu(product(hidden, w2h, w2l))
        hidden = silu(product(hidden, w3h, w3l))
        result = product(hidden, w4h, w4l)
        answer[pl.ds(group * GROUP, GROUP)] = result.reshape(GROUP, CAP, FEATURES)
        for part in range(TURNS):
            for lane in range(8):
                turn_number = group * TURNS + part
                step = turn_number * 8 + lane
                other = source(turn_number, lane)
                if part == 0 and lane == 0:

                    @pl.when(group > 0)
                    def _():
                        back(step, other).start()
                else:
                    back(step, other).start()
        return carry

    def arrived(first, count, group):
        pltpu.make_async_remote_copy(
            src_ref=recv.at[pl.ds(first, count)],
            dst_ref=recv.at[pl.ds(first, count)],
            send_sem=out_send,
            recv_sem=out_recv.at[group],
            device_id=me,
            device_id_type=LOGICAL,
        ).wait_recv()

    def arrived_network(group, carry):
        @pl.when(group == 0)
        def _():
            arrived(1, GROUP - 1, 0)

        @pl.when(group > 0)
        def _():
            arrived(group * GROUP, GROUP, group)

        @pl.when(group < GROUPS - AHEAD)
        def _():
            first = (group + AHEAD) * TURNS
            lax.fori_loop(first, first + TURNS, dispatch, 0)

        network(group, carry)

        @pl.when(group == GROUPS - 2)
        def _():
            receive_halo()
            lax.fori_loop(0, ROWS_X // 4, widen, 0)


        return carry

    lax.fori_loop(0, GROUPS, arrived_network, 0)
    own_answer = pltpu.make_async_copy(answer.at[0], drag_hbm.at[me], own_sem)
    own_answer.start()
    diffuse(0)
    diffuse(1)
    diffuse(2)
    diffuse(3)
    diffused = pltpu.make_async_copy(profiles, diffused_hbm, diffused_sem)
    diffused.start()

    others = DEVICES - 1
    pltpu.make_async_remote_copy(
        src_ref=answer.at[pl.ds(0, others)],
        dst_ref=drag_hbm.at[pl.ds(0, others)],
        send_sem=back_send,
        recv_sem=back_recv,
        device_id=me,
        device_id_type=LOGICAL,
    ).wait()
    pltpu.make_async_remote_copy(
        src_ref=send.at[pl.ds(0, others)],
        dst_ref=recv.at[pl.ds(0, others)],
        send_sem=out_send,
        recv_sem=out_recv.at[0],
        device_id=me,
        device_id_type=LOGICAL,
    ).wait_send()
    diffused.wait()
    own_answer.wait()


def drag_and_diffusion(regimes, active_columns, u_field, v_field, diffusivity, layers):
    vmem = pl.BlockSpec(memory_space=pltpu.VMEM)
    hbm = pl.BlockSpec(memory_space=pltpu.HBM)
    shapes = [layer.shape[1:] for layer in layers]
    halves = [pltpu.VMEM(shape, BF16) for shape in shapes for _ in range(2)]
    dma = pltpu.SemaphoreType.DMA
    return pl.pallas_call(
        main_kernel,
        out_shape=(
            jax.ShapeDtypeStruct((DEVICES, CAP, FEATURES), F32),
            jax.ShapeDtypeStruct((WX * WY, FEATURES), F32),
            jax.ShapeDtypeStruct((1, ACTIVE), jnp.int32),
        ),
        in_specs=[vmem, vmem] + [hbm] * 7,
        out_specs=(hbm, hbm, vmem),
        scratch_shapes=[
            pltpu.VMEM((CAP, DEVICES), jnp.int32),
            pltpu.SMEM((CAP, DEVICES), jnp.int32),
            pltpu.VMEM((2, LEVELS, PADDED, WY), F32),
            pltpu.VMEM((WX * WY, FEATURES), F32),
            pltpu.VMEM((2, ROWS_X, ROWS_Y, FEATURES), F32),
            pltpu.VMEM((3, WX + 16, WY), F32),
            pltpu.VMEM((16, WY), F32),
            pltpu.VMEM((ROWS_X, ROWS_Y, FEATURES), F32),
            pltpu.VMEM((DEVICES, CAP, FEATURES), F32),
            pltpu.VMEM((DEVICES, CAP, FEATURES), F32),
            pltpu.VMEM((DEVICES, CAP, FEATURES), F32),
            *[pltpu.VMEM(shape, F32) for shape in shapes],
            *halves,
            dma((4, 2)),
            dma,
            dma((4,)),
            dma((8,)),
            dma((8,)),
            dma((8,)),
            dma((8,)),
            dma,
            dma((GROUPS,)),
            dma,
            dma,
            dma,
            dma,
        ],
        compiler_params=pltpu.CompilerParams(
            collective_id=0, has_side_effects=True, vmem_limit_bytes=59840 << 10
        ),
    )(regimes.reshape(1, ACTIVE), active_columns.reshape(1, ACTIVE), u_field, v_field, diffusivity, *layers)


def place_kernel(
    column_ref, slot_ref, drag_hbm, diffused_hbm, u_hbm, v_hbm, drag, dense, diffused, staged, drag_sem, in_sem, out_sem
):
    pieces = 4
    wide = WX // pieces
    drag_load = pltpu.make_async_copy(drag_hbm, drag, drag_sem)
    drag_load.start()
    loads = []
    for piece in range(pieces):
        part = pl.ds(piece * wide * WY, wide * WY)
        load = pltpu.make_async_copy(diffused_hbm.at[part], diffused.at[part], in_sem.at[piece])
        loads.append(load)

    def clear(x, carry):
        dense[pl.ds(pl.multiple_of(x * WY, WY), WY), :] = jnp.zeros((WY, FEATURES), F32)
        return carry

    lax.fori_loop(0, WX, clear, 0)
    drag_load.wait()
    for load in loads:
        load.start()
    drags = drag.reshape(DEVICES * CAP, FEATURES)

    def place(step, carry):
        rows = [drags[pl.ds(slot_ref[0, step * 32 + k], 1), :] for k in range(32)]
        for k in range(32):
            dense[pl.ds(column_ref[step * 32 + k], 1), :] = rows[k]
        return carry

    lax.fori_loop(0, ACTIVE // 32, place, 0)
    flat = staged.reshape(2 * LEVELS * PADDED, WY)

    def turn(step, carry):
        for k in range(8):
            x = 8 * step + k
            part = pl.ds(pl.multiple_of(x * WY, WY), WY)
            block = dense[part, :] + diffused[part, :]
            flat[pl.ds(x, FEATURES, stride=PADDED), :] = block.T
        return carry

    copies = []
    for piece in range(pieces):
        loads[piece].wait()
        lax.fori_loop(piece * wide // 8, (piece + 1) * wide // 8, turn, 0)
        part = pl.ds(piece * wide, wide)
        for which, target in enumerate((u_hbm, v_hbm)):
            copy = pltpu.make_async_copy(staged.at[which, :, part, :], target.at[:, part, :], out_sem.at[piece, which])
            copy.start()
            copies.append(copy)
    for copy in copies:
        copy.wait()


def place_drag(active_columns, slots, drag, diffused):
    smem = pl.BlockSpec(memory_space=pltpu.SMEM)
    hbm = pl.BlockSpec(memory_space=pltpu.HBM)
    shape = jax.ShapeDtypeStruct((LEVELS, WX, WY), F32)
    return pl.pallas_call(
        place_kernel,
        out_shape=(shape, shape),
        in_specs=[smem, smem, hbm, hbm],
        out_specs=(hbm, hbm),
        scratch_shapes=[
            pltpu.VMEM((DEVICES, CAP, FEATURES), F32),
            pltpu.VMEM((WX * WY, FEATURES), F32),
            pltpu.VMEM((WX * WY, FEATURES), F32),
            pltpu.VMEM((2, LEVELS, PADDED, WY), F32),
            pltpu.SemaphoreType.DMA,
            pltpu.SemaphoreType.DMA((4,)),
            pltpu.SemaphoreType.DMA((4, 2)),
        ],
        compiler_params=pltpu.CompilerParams(vmem_limit_bytes=59840 << 10),
    )(active_columns, slots, drag, diffused)


def body(
    u_field,
    v_field,
    diffusivity,
    active_columns,
    regimes,
    first_layer,
    second_layer,
    third_layer,
    last_layer,
):
    layers = (first_layer, second_layer, third_layer, last_layer)
    drag, diffused, slots = drag_and_diffusion(regimes, active_columns, u_field, v_field, diffusivity, layers)
    return place_drag(active_columns, slots, drag, diffused)


def solution(mesh):
    in_specs = (
        P(None, "tile", "inf"),
        P(None, "tile", "inf"),
        P("tile", "inf"),
        P(("tile", "inf")),
        P(("tile", "inf"), None),
        P(("tile", "inf"), None, None),
        P(("tile", "inf"), None, None),
        P(("tile", "inf"), None, None),
        P(("tile", "inf"), None, None),
    )
    out_specs = (P(None, "tile", "inf"), P(None, "tile", "inf"))
    return jax.shard_map(body, mesh=mesh, in_specs=in_specs, out_specs=out_specs, check_vma=False)
```
